1024 devices in a mesh: rep: 8 (over z_lo), table: 32 (over z_hi, y, core), tensor: 4 (over x).
Axes of the slice: x: 4, y: 4, z: 32 (z_hi: 4, z_lo: 8; z = z_hi * 8 + z_lo), core: 2. Of those that a mesh axis runs over, the one named last changes fastest.
Arguments:
- pooled: bfloat16 [2048, 256, 192], P('rep', 'table'), may hold values from -6 to 6
- lc_weight: bfloat16 [256, 256], P('tensor'), may hold values from -0.375 to 0.375
- fm_proj: bfloat16 [256, 256], P(None, 'tensor'), may hold values from -0.375 to 0.375
- fm_out: bfloat16 [256, 192], P('tensor'), may hold values from -0.02734375 to 0.02734375
- cotangent: bfloat16 [2048, 256, 192], P(('rep', 'table')), may hold values from -6 to 6
Outputs:
- layer_out: bfloat16 [2048, 256, 192], P(('rep', 'table'))
- emb_grad: bfloat16 [2048, 256, 192], P('rep', 'table', 'tensor')
- lc_grad: float32 [256, 256], P('tensor')
- proj_grad: float32 [256, 256], P(None, 'tensor')
- out_grad: float32 [256, 192], P('tensor')
The draws below stay inside these ranges and needn't reach their ends.
All inputs are finite; a program needn't handle non-finite values.
Results may differ from the reference program's by a relative error of at most 0.015.
Values may be sent and summed in bfloat16 or wider, within the bound.
No kernel may reach another device: no remote copies, remote signals or barrier semaphores. Data moves between devices by JAX's collectives and lax.ppermute only.
A program may use at most 32 MiB of HBM per device.

```python
import jax
import jax.numpy as jnp
from jax import lax

NEMB = 256
D = 192
K = 256
SAMP = 8
BATCH = 2048
N_TENSOR = 4


def steps_of(key, dims, pieces, smallest, largest):
    factor_of = 1.0
    for axis_at, shards_of in pieces:
        steps = jax.random.uniform(jax.random.fold_in(jax.random.fold_in(key, 6), axis_at), (shards_of,), jnp.float32, smallest / len(pieces), largest / len(pieces))
        factor_of = factor_of * jnp.repeat(jnp.exp(steps), dims[axis_at] // shards_of).reshape((-1,) + (1,) * (len(dims) - 1 - axis_at))
    return factor_of


def bell_draw(stream_key, dims, width, bound, split=(), kind=jnp.bfloat16):
    entries = width * jax.random.normal(stream_key, dims, jnp.float32)
    if split:
        entries = entries * steps_of(stream_key, dims, split, -0.22, 0.18)
    return jnp.clip(entries, -bound, bound).astype(kind)


def setup_inputs(seed: int = 0) -> dict:
    splits = jax.random.split(jax.random.key(seed), 6)
    return {
        "pooled": bell_draw(splits[0], (BATCH, NEMB, D), 1.0, 6.0, ((0, 8), (1, 32))),
        "lc_weight": bell_draw(splits[1], (NEMB, NEMB), NEMB ** -0.5, 0.375, ((0, 4),)),
        "fm_proj": bell_draw(splits[2], (NEMB, K), NEMB ** -0.5, 0.375, ((1, 4),)),
        "fm_out": bell_draw(splits[3], (K, D), (K * D) ** -0.5, 0.02734375, ((0, 4),)),
        "cotangent": bell_draw(splits[4], (BATCH, NEMB, D), 1.0, 6.0, ((0, 256),)),
    }


def quarter_terms(embeds, upstream, proj_part, out_part, lc_part, row_start):
    row_count = lc_part.shape[0]
    embeds_wide = embeds.astype(jnp.float32)
    upstream_wide = upstream.astype(jnp.float32)
    compressed = jnp.einsum('snd,nk->sdk', embeds_wide, proj_part.astype(jnp.float32)).astype(jnp.bfloat16)
    interact = jnp.einsum('snd,sdk->snk', embeds_wide, compressed.astype(jnp.float32)).astype(jnp.bfloat16)
    own_rows = embeds_wide[:, row_start:row_start + row_count]
    forward_term = jnp.einsum('snk,kd->snd', interact.astype(jnp.float32), out_part.astype(jnp.float32))
    forward_term = forward_term + jnp.einsum('sjd,jm->smd', own_rows, lc_part.astype(jnp.float32))
    interact_grad = jnp.einsum('snd,kd->snk', upstream_wide, out_part.astype(jnp.float32)).astype(jnp.bfloat16)
    compress_grad = jnp.einsum('snd,snk->sdk', embeds_wide, interact_grad.astype(jnp.float32)).astype(jnp.bfloat16)
    input_grad = jnp.einsum('snk,sdk->snd', interact_grad.astype(jnp.float32), compressed.astype(jnp.float32))
    input_grad = input_grad + jnp.einsum('nk,sdk->snd', proj_part.astype(jnp.float32), compress_grad.astype(jnp.float32))
    lc_rows = jnp.einsum('jm,smd->sjd', lc_part.astype(jnp.float32), upstream_wide) + upstream_wide[:, row_start:row_start + row_count]
    input_grad = input_grad.at[:, row_start:row_start + row_count].add(lc_rows)
    out_term = jnp.einsum('snk,snd->kd', interact.astype(jnp.float32), upstream_wide)
    proj_term = jnp.einsum('snd,sdk->nk', embeds_wide, compress_grad.astype(jnp.float32))
    lc_term = jnp.einsum('sjd,smd->jm', own_rows, upstream_wide)
    return forward_term, input_grad, out_term, proj_term, lc_term


def reference(pooled, lc_weight, fm_proj, fm_out, cotangent):
    key_count = K // N_TENSOR
    row_count = NEMB // N_TENSOR
    block_total = BATCH // SAMP
    embed_blocks = pooled.reshape(block_total, SAMP, NEMB, D)
    upstream_blocks = cotangent.reshape(block_total, SAMP, NEMB, D)

    def sample_step(totals, sample_pair):
        embeds, upstream = sample_pair
        mixture = jnp.zeros((SAMP, NEMB, D), jnp.float32)
        input_grad = jnp.zeros((SAMP, NEMB, D), jnp.float32)
        out_blocks = []
        proj_blocks = []
        lc_blocks = []
        for segment in range(N_TENSOR):
            keys = slice(segment * key_count, (segment + 1) * key_count)
            rows = slice(segment * row_count, (segment + 1) * row_count)
            block_terms = quarter_terms(embeds, upstream, fm_proj[:, keys], fm_out[keys], lc_weight[rows], segment * row_count)
            mixture = mixture + lax.optimization_barrier(block_terms[0].astype(jnp.bfloat16)).astype(jnp.float32)
            input_grad = input_grad + block_terms[1]
            out_blocks.append(block_terms[2])
            proj_blocks.append(block_terms[3])
            lc_blocks.append(block_terms[4])
        layer_rows = (embeds.astype(jnp.float32) + mixture).astype(jnp.bfloat16)
        totals = (totals[0] + jnp.concatenate(out_blocks, 0),
                  totals[1] + jnp.concatenate(proj_blocks, 1),
                  totals[2] + jnp.concatenate(lc_blocks, 0))
        return totals, (layer_rows, input_grad.astype(jnp.bfloat16))

    start_totals = (jnp.zeros((K, D), jnp.float32), jnp.zeros((NEMB, K), jnp.float32), jnp.zeros((NEMB, NEMB), jnp.float32))
    totals, stacked = lax.scan(sample_step, start_totals, (embed_blocks, upstream_blocks))
    wide_scale = float(BATCH * D) ** -0.5
    out_scale = float(BATCH * NEMB * D) ** -0.5
    layer_out = stacked[0].reshape(BATCH, NEMB, D)
    emb_grad = stacked[1].reshape(BATCH, NEMB, D)
    return (layer_out, emb_grad, totals[2] * wide_scale, totals[1] * wide_scale, totals[0] * out_scale)
```

```python
import jax
import jax.numpy as jnp
from jax import lax
from jax.experimental import pallas as pl
from jax.experimental.pallas import tpu as pltpu
from jax.sharding import Mesh, PartitionSpec as P

BF = jnp.bfloat16
F32 = jnp.float32
TABLE = ("zhi", "y", "core")
PLANE = ("y", "core", "x")
COLUMN = ("y", "core")
VMEM_BYTES = 48 * 1024 * 1024


def dot(a, b):
    return lax.dot_general(a, b, (((1,), (0,)), ((), ())), preferred_element_type=F32)


def dot_t(a, b):
    return lax.dot_general(a, b, (((1,), (1,)), ((), ())), preferred_element_type=F32)


def params():
    return pltpu.CompilerParams(vmem_limit_bytes=VMEM_BYTES)


def whole(shape):
    zeros = (0,) * len(shape)
    return pl.BlockSpec(shape, lambda i, t: zeros)


def pack_kernel(t_ref, pooled_ref, out_ref):
    first = pooled_ref[:, 0, 0].astype(F32)
    second = pooled_ref[:, 0, 1].astype(F32)
    n = first.shape[0]
    mixed = jnp.concatenate([first[:, :, 128:], second[:, :, 128:]], axis=2)
    rows = jnp.concatenate([first[:, :, :128], second[:, :, :128], mixed], axis=1)
    out_ref[...] = rows.astype(BF).reshape(n, 24, 128)


def pack_rows(t, pooled):
    view = pooled.reshape(32, 4, 2, 8, 192)
    return pl.pallas_call(
        pack_kernel,
        grid_spec=pltpu.PrefetchScalarGridSpec(
            num_scalar_prefetch=1,
            grid=(1,),
            in_specs=[pl.BlockSpec((32, 1, 2, 8, 192), lambda i, t: (0, t[0], 0, 0, 0))],
            out_specs=whole((32, 24, 128)),
        ),
        out_shape=jax.ShapeDtypeStruct((32, 24, 128), BF),
        compiler_params=params(),
        name="pack_rows",
    )(t, view)


def upstream_kernel(t_ref, g_ref, w_ref, ig_ref, igt_ref, base_ref, wt_ref, p_ref):
    lc = w_ref[:, :256]
    pt = w_ref[:, 256:512]
    out_w = w_ref[:, 512:704]
    wt_ref[...] = lc.astype(F32).T.astype(BF)
    p_ref[...] = pt.astype(F32).T.astype(BF)
    for s in range(2):
        g = g_ref[s]
        ig_ref[s] = dot_t(g, out_w).astype(BF)
        igt_ref[s] = dot_t(out_w, g).astype(BF)
        base_ref[s] = g.astype(F32) + dot(lc, g)


def upstream_terms(t, cotangent, weights):
    return pl.pallas_call(
        upstream_kernel,
        grid_spec=pltpu.PrefetchScalarGridSpec(
            num_scalar_prefetch=1,
            grid=(1,),
            in_specs=[
                pl.BlockSpec((2, 256, 192), lambda i, t: (t[0], 0, 0)),
                whole((256, 704)),
            ],
            out_specs=[
                whole((2, 256, 256)),
                whole((2, 256, 256)),
                whole((2, 256, 192)),
                whole((256, 256)),
                whole((256, 256)),
            ],
        ),
        out_shape=[
            jax.ShapeDtypeStruct((2, 256, 256), BF),
            jax.ShapeDtypeStruct((2, 256, 256), BF),
            jax.ShapeDtypeStruct((2, 256, 192), F32),
            jax.ShapeDtypeStruct((256, 256), BF),
            jax.ShapeDtypeStruct((256, 256), BF),
        ],
        compiler_params=params(),
        name="upstream_terms",
    )(t, cotangent, weights)


def layer_kernel(t_ref, x_ref, g_ref, w_ref, ig_ref, igt_ref, base_ref, wt_ref, p_ref, layer_ref, msg_ref):
    pt = w_ref[:, 256:512]
    out_w = w_ref[:, 512:704]
    wt = wt_ref[...]
    planes = x_ref[...].astype(F32)
    plane = [planes[:, 8 * i : 8 * i + 8].reshape(256, 128) for i in range(3)]
    xs = [
        jnp.concatenate([plane[0], plane[2][:, :64]], axis=1),
        jnp.concatenate([plane[1], plane[2][:, 64:]], axis=1),
    ]
    grads = []
    out_sum = proj_sum = lc_sum = None
    for s in range(2):
        x32 = xs[s]
        x = x32.astype(BF)
        g = g_ref[s]
        ct = dot(pt, x).astype(BF)
        inter = dot_t(x, ct).astype(BF)
        inter_t = dot_t(ct, x).astype(BF)
        forward = dot(inter, out_w) + dot(wt, x)
        layer_ref[s] = (x32 + forward).astype(BF)
        cgt = dot(igt_ref[s], x).astype(BF)
        grads.append(base_ref[s] + dot(ig_ref[s], ct) + dot(p_ref[...], cgt))
        out_term, proj_term, lc_term = dot(inter_t, g), dot_t(cgt, x), dot_t(x, g)
        out_sum = out_term if s == 0 else out_sum + out_term
        proj_sum = proj_term if s == 0 else proj_sum + proj_term
        lc_sum = lc_term if s == 0 else lc_sum + lc_term
    pad = jnp.zeros((256, 32), F32)
    emb = [
        jnp.concatenate([grads[0][:, 48 * q : 48 * q + 48], grads[1][:, 48 * q : 48 * q + 48], pad], axis=1)
        for q in range(4)
    ]
    out_tail = jnp.concatenate([out_sum[:, 128:], jnp.zeros((256, 64), F32)], axis=1)
    for c in range(8):
        for q in range(4):
            rows = slice(64 * q + 8 * c, 64 * q + 8 * c + 8)
            tiles = [emb[q][64 * z + 8 * c : 64 * z + 8 * c + 8] for z in range(4)]
            tiles += [lc_sum[rows, :128], lc_sum[rows, 128:]]
            tiles += [proj_sum[rows, :128], proj_sum[rows, 128:]]
            tiles += [out_sum[rows, :128], out_tail[rows]]
            msg_ref[4 * c + q] = jnp.concatenate(tiles, axis=0).astype(BF)


def layer_terms(t, rows, cotangent, weights, ig, igt, base, wt, p):
    return pl.pallas_call(
        layer_kernel,
        grid_spec=pltpu.PrefetchScalarGridSpec(
            num_scalar_prefetch=1,
            grid=(1,),
            in_specs=[
                whole((32, 24, 128)),
                pl.BlockSpec((2, 256, 192), lambda i, t: (t[0], 0, 0)),
                whole((256, 704)),
                whole((2, 256, 256)),
                whole((2, 256, 256)),
                whole((2, 256, 192)),
                whole((256, 256)),
                whole((256, 256)),
            ],
            out_specs=[whole((2, 256, 192)), whole((32, 80, 128))],
        ),
        out_shape=[
            jax.ShapeDtypeStruct((2, 256, 192), BF),
            jax.ShapeDtypeStruct((32, 80, 128), BF),
        ],
        compiler_params=params(),
        name="layer_terms",
    )(t, rows, cotangent, weights, ig, igt, base, wt, p)


def plane_kernel(in_ref, out_ref):
    total = in_ref[0, 32:80].astype(F32)
    for d in range(1, 32):
        total = total + in_ref[d, 32:80].astype(F32)
    total = total.astype(BF)
    wide = []
    for c in range(8):
        parts = [in_ref[4 * c + q, 0:32].astype(F32)[:, :96] for q in range(4)]
        wide.append(jnp.concatenate(parts, axis=1))
    for z in range(4):
        rows = jnp.concatenate([wide[c][8 * z : 8 * z + 8] for c in range(8)], axis=0).astype(BF)
        for i in range(3):
            out_ref[z, 64 * i : 64 * i + 64] = rows[:, 128 * i : 128 * i + 128]
        out_ref[z, 192:240] = total


def plane_terms(received):
    return pl.pallas_call(
        plane_kernel,
        out_shape=jax.ShapeDtypeStruct((4, 240, 128), BF),
        compiler_params=params(),
        name="plane_terms",
    )(received)


def column_kernel(in_ref, emb_ref, total_ref):
    total = in_ref[0, 192:240].astype(F32)
    for z in range(1, 4):
        total = total + in_ref[z, 192:240].astype(F32)
    total_ref[...] = total
    for z in range(4):
        planes = [in_ref[z, 64 * i : 64 * i + 64].astype(F32) for i in range(3)]
        rows = jnp.concatenate(planes, axis=1).reshape(8, 8, 384)
        for i in range(8):
            emb_ref[8 * z : 8 * z + 8, i] = rows[:, :, 48 * i : 48 * i + 48].astype(BF)


def column_terms(received):
    return pl.pallas_call(
        column_kernel,
        out_shape=[
            jax.ShapeDtypeStruct((32, 8, 8, 48), BF),
            jax.ShapeDtypeStruct((48, 128), F32),
        ],
        compiler_params=params(),
        name="column_terms",
    )(received)


def final_kernel(wide_scale, out_scale, in_ref, lc_ref, proj_ref, out_ref):
    rows = [in_ref[c] for c in range(8)]
    part = [jnp.concatenate([r[8 * i : 8 * i + 8] for r in rows], axis=0) for i in range(6)]
    lc_ref[...] = jnp.concatenate(part[0:2], axis=1) * wide_scale
    proj_ref[...] = jnp.concatenate([part[2].T, part[3].T], axis=0) * wide_scale
    out_ref[...] = jnp.concatenate([part[4], part[5][:, :64]], axis=1) * out_scale


def final_terms(received, wide_scale, out_scale):
    def kernel(*refs):
        final_kernel(wide_scale, out_scale, *refs)

    return pl.pallas_call(
        kernel,
        out_shape=[
            jax.ShapeDtypeStruct((64, 256), F32),
            jax.ShapeDtypeStruct((256, 64), F32),
            jax.ShapeDtypeStruct((64, 192), F32),
        ],
        compiler_params=params(),
        name="final_terms",
    )(received)


def spread(block, axes, count):
    copies = jnp.broadcast_to(block[None], (count,) + block.shape)
    return lax.all_to_all(copies, axes, split_axis=0, concat_axis=0, tiled=True)


def shards(pooled, lc_weight, fm_proj, fm_out, cotangent):
    t = lax.axis_index("x").astype(jnp.int32)[None]
    rep_count = lax.axis_size("zlo")
    sample_total = cotangent.shape[0] * rep_count * 32
    wide_scale = float(sample_total * 192) ** (-0.5)
    out_scale = float(sample_total * 256 * 192) ** (-0.5)
    sent = pack_rows(t, pooled)
    rows = lax.all_to_all(sent, TABLE, split_axis=0, concat_axis=0, tiled=True)
    own = jnp.concatenate([lc_weight, fm_proj.T, fm_out], axis=1)
    weights = spread(own, "x", 4).reshape(256, 704)
    ig, igt, base, wt, p = upstream_terms(t, cotangent, weights)
    layer, messages = layer_terms(t, rows, cotangent, weights, ig, igt, base, wt, p)
    plane = lax.all_to_all(messages, PLANE, split_axis=0, concat_axis=0, tiled=True)
    column = plane_terms(plane)
    column = lax.all_to_all(column, "zhi", split_axis=0, concat_axis=0, tiled=True)
    emb_grad, total = column_terms(column)
    total = jnp.sum(spread(total, "zlo", rep_count), axis=0)
    lc_grad, proj_grad, out_grad = final_terms(spread(total, COLUMN, 8), wide_scale, out_scale)
    layer_out = spread(layer, "x", 4).reshape(8, 256, 192)
    return (layer_out, emb_grad.reshape(256, 8, 48), lc_grad, proj_grad, out_grad)


def solution(mesh):
    reps = mesh.shape["rep"]
    fine = Mesh(mesh.devices.reshape(reps, 4, 4, 2, 4), ("zlo", "zhi", "y", "core", "x"))
    in_specs = (
        P("zlo", TABLE, None),
        P("x", None),
        P(None, "x"),
        P("x", None),
        P(("zlo",) + TABLE, None, None),
    )
    out_specs = (
        P(("zlo",) + TABLE, None, None),
        P("zlo", TABLE, "x"),
        P("x", None),
        P(None, "x"),
        P("x", None),
    )
    return jax.shard_map(shards, mesh=fine, in_specs=in_specs, out_specs=out_specs, check_vma=False)
```

```python
import jax
import jax.numpy as jnp
from jax import lax
from jax.experimental import pallas as pl
from jax.experimental.pallas import tpu as pltpu
from jax.sharding import Mesh, PartitionSpec as P

BF = jnp.bfloat16
F32 = jnp.float32
TABLE = ("zhi", "y", "core")
PLANE = ("y", "core", "x")
COLUMN = ("y", "core")
VMEM_BYTES = 48 * 1024 * 1024


def dot(a, b):
    return lax.dot_general(a, b, (((1,), (0,)), ((), ())), preferred_element_type=F32)


def dot_t(a, b):
    return lax.dot_general(a, b, (((1,), (1,)), ((), ())), preferred_element_type=F32)


def params():
    return pltpu.CompilerParams(vmem_limit_bytes=VMEM_BYTES)


def whole(shape):
    zeros = (0,) * len(shape)
    return pl.BlockSpec(shape, lambda i, t: zeros)


def pack_kernel(t_ref, pooled_ref, out_ref):
    first = pooled_ref[:, 0, 0].astype(F32)
    second = pooled_ref[:, 0, 1].astype(F32)
    n = first.shape[0]
    mixed = jnp.concatenate([first[:, :, 128:], second[:, :, 128:]], axis=2)
    rows = jnp.concatenate([first[:, :, :128], second[:, :, :128], mixed], axis=1)
    out_ref[...] = rows.astype(BF).reshape(n, 24, 128)


def pack_rows(t, pooled):
    view = pooled.reshape(32, 4, 2, 8, 192)
    return pl.pallas_call(
        pack_kernel,
        grid_spec=pltpu.PrefetchScalarGridSpec(
            num_scalar_prefetch=1,
            grid=(1,),
            in_specs=[pl.BlockSpec((32, 1, 2, 8, 192), lambda i, t: (0, t[0], 0, 0, 0))],
            out_specs=whole((32, 24, 128)),
        ),
        out_shape=jax.ShapeDtypeStruct((32, 24, 128), BF),
        compiler_params=params(),
        name="pack_rows",
    )(t, view)


def upstream_kernel(t_ref, g_ref, w_ref, ig_ref, igt_ref, base_ref, wt_ref, p_ref):
    lc = w_ref[:, :256]
    pt = w_ref[:, 256:512]
    out_w = w_ref[:, 512:704]
    wt_ref[...] = lc.astype(F32).T.astype(BF)
    p_ref[...] = pt.astype(F32).T.astype(BF)
    for s in range(2):
        g = g_ref[s]
        ig_ref[s] = dot_t(g, out_w).astype(BF)
        igt_ref[s] = dot_t(out_w, g).astype(BF)
        base_ref[s] = g.astype(F32) + dot(lc, g)


def upstream_terms(t, cotangent, weights):
    return pl.pallas_call(
        upstream_kernel,
        grid_spec=pltpu.PrefetchScalarGridSpec(
            num_scalar_prefetch=1,
            grid=(1,),
            in_specs=[
                pl.BlockSpec((2, 256, 192), lambda i, t: (t[0], 0, 0)),
                whole((256, 704)),
            ],
            out_specs=[
                whole((2, 256, 256)),
                whole((2, 256, 256)),
                whole((2, 256, 192)),
                whole((256, 256)),
                whole((256, 256)),
            ],
        ),
        out_shape=[
            jax.ShapeDtypeStruct((2, 256, 256), BF),
            jax.ShapeDtypeStruct((2, 256, 256), BF),
            jax.ShapeDtypeStruct((2, 256, 192), F32),
            jax.ShapeDtypeStruct((256, 256), BF),
            jax.ShapeDtypeStruct((256, 256), BF),
        ],
        compiler_params=params(),
        name="upstream_terms",
    )(t, cotangent, weights)


def layer_kernel(t_ref, x_ref, g_ref, w_ref, ig_ref, igt_ref, base_ref, wt_ref, p_ref, layer_ref, msg_ref):
    pt = w_ref[:, 256:512]
    out_w = w_ref[:, 512:704]
    wt = wt_ref[...]
    planes = x_ref[...].astype(F32)
    plane = [planes[:, 8 * i : 8 * i + 8].reshape(256, 128) for i in range(3)]
    xs = [
        jnp.concatenate([plane[0], plane[2][:, :64]], axis=1),
        jnp.concatenate([plane[1], plane[2][:, 64:]], axis=1),
    ]
    grads = []
    out_sum = proj_sum = lc_sum = None
    for s in range(2):
        x32 = xs[s]
        x = x32.astype(BF)
        g = g_ref[s]
        ct = dot(pt, x).astype(BF)
        inter = dot_t(x, ct).astype(BF)
        inter_t = dot_t(ct, x).astype(BF)
        forward = dot(inter, out_w) + dot(wt, x)
        layer_ref[s] = (x32 + forward).astype(BF)
        cgt = dot(igt_ref[s], x).astype(BF)
        grads.append(base_ref[s] + dot(ig_ref[s], ct) + dot(p_ref[...], cgt))
        out_term, proj_term, lc_term = dot(inter_t, g), dot_t(cgt, x), dot_t(x, g)
        out_sum = out_term if s == 0 else out_sum + out_term
        proj_sum = proj_term if s == 0 else proj_sum + proj_term
        lc_sum = lc_term if s == 0 else lc_sum + lc_term
    pad = jnp.zeros((256, 32), F32)
    emb = [
        jnp.concatenate([grads[0][:, 48 * q : 48 * q + 48], grads[1][:, 48 * q : 48 * q + 48], pad], axis=1)
        for q in range(4)
    ]
    out_tail = jnp.concatenate([out_sum[:, 128:], jnp.zeros((256, 64), F32)], axis=1)
    for c in range(8):
        for q in range(4):
            rows = slice(64 * q + 8 * c, 64 * q + 8 * c + 8)
            tiles = [emb[q][64 * z + 8 * c : 64 * z + 8 * c + 8] for z in range(4)]
            tiles += [lc_sum[rows, :128], lc_sum[rows, 128:]]
            tiles += [proj_sum[rows, :128], proj_sum[rows, 128:]]
            tiles += [out_sum[rows, :128], out_tail[rows]]
            msg_ref[4 * c + q] = jnp.concatenate(tiles, axis=0).astype(BF)


def layer_terms(t, rows, cotangent, weights, ig, igt, base, wt, p):
    return pl.pallas_call(
        layer_kernel,
        grid_spec=pltpu.PrefetchScalarGridSpec(
            num_scalar_prefetch=1,
            grid=(1,),
            in_specs=[
                whole((32, 24, 128)),
                pl.BlockSpec((2, 256, 192), lambda i, t: (t[0], 0, 0)),
                whole((256, 704)),
                whole((2, 256, 256)),
                whole((2, 256, 256)),
                whole((2, 256, 192)),
                whole((256, 256)),
                whole((256, 256)),
            ],
            out_specs=[whole((2, 256, 192)), whole((32, 80, 128))],
        ),
        out_shape=[
            jax.ShapeDtypeStruct((2, 256, 192), BF),
            jax.ShapeDtypeStruct((32, 80, 128), BF),
        ],
        compiler_params=params(),
        name="layer_terms",
    )(t, rows, cotangent, weights, ig, igt, base, wt, p)


def plane_kernel(in_ref, out_ref):
    total = in_ref[0, 32:80].astype(F32)
    for d in range(1, 32):
        total = total + in_ref[d, 32:80].astype(F32)
    total = total.astype(BF)
    wide = []
    for c in range(8):
        parts = [in_ref[4 * c + q, 0:32].astype(F32)[:, :96] for q in range(4)]
        wide.append(jnp.concatenate(parts, axis=1))
    for z in range(4):
        rows = jnp.concatenate([wide[c][8 * z : 8 * z + 8] for c in range(8)], axis=0).astype(BF)
        for i in range(3):
            out_ref[z, 64 * i : 64 * i + 64] = rows[:, 128 * i : 128 * i + 128]
        out_ref[z, 192:240] = total


def plane_terms(received):
    return pl.pallas_call(
        plane_kernel,
        out_shape=jax.ShapeDtypeStruct((4, 240, 128), BF),
        compiler_params=params(),
        name="plane_terms",
    )(received)


def column_kernel(in_ref, emb_ref, total_ref):
    total = in_ref[0, 192:240].astype(F32)
    for z in range(1, 4):
        total = total + in_ref[z, 192:240].astype(F32)
    for r in range(total_ref.shape[0]):
        total_ref[r] = total.astype(BF)
    for z in range(4):
        planes = [in_ref[z, 64 * i : 64 * i + 64].astype(F32) for i in range(3)]
        rows = jnp.concatenate(planes, axis=1).reshape(8, 8, 384)
        for i in range(8):
            emb_ref[8 * z : 8 * z + 8, i] = rows[:, :, 48 * i : 48 * i + 48].astype(BF)


def column_terms(received, rep_count):
    return pl.pallas_call(
        column_kernel,
        out_shape=[
            jax.ShapeDtypeStruct((32, 8, 8, 48), BF),
            jax.ShapeDtypeStruct((rep_count, 48, 128), BF),
        ],
        compiler_params=params(),
        name="column_terms",
    )(received)


def replica_kernel(in_ref, out_ref):
    total = in_ref[0].astype(F32)
    for r in range(1, in_ref.shape[0]):
        total = total + in_ref[r].astype(F32)
    for c in range(8):
        out_ref[c] = total


def replica_terms(received):
    return pl.pallas_call(
        replica_kernel,
        out_shape=jax.ShapeDtypeStruct((8, 48, 128), F32),
        compiler_params=params(),
        name="replica_terms",
    )(received)


def final_kernel(wide_scale, out_scale, in_ref, lc_ref, proj_ref, out_ref):
    rows = [in_ref[c] for c in range(8)]
    part = [jnp.concatenate([r[8 * i : 8 * i + 8] for r in rows], axis=0) for i in range(6)]
    lc_ref[...] = jnp.concatenate(part[0:2], axis=1) * wide_scale
    proj_ref[...] = jnp.concatenate(part[2:4], axis=1) * wide_scale
    out_ref[...] = jnp.concatenate([part[4], part[5][:, :64]], axis=1) * out_scale


def final_terms(received, wide_scale, out_scale):
    def kernel(*refs):
        final_kernel(wide_scale, out_scale, *refs)

    return pl.pallas_call(
        kernel,
        out_shape=[
            jax.ShapeDtypeStruct((64, 256), F32),
            jax.ShapeDtypeStruct((64, 256), F32),
            jax.ShapeDtypeStruct((64, 192), F32),
        ],
        compiler_params=params(),
        name="final_terms",
    )(received)


def swap(blocks, axes):
    return lax.all_to_all(blocks, axes, split_axis=0, concat_axis=0, tiled=True)


def shards(pooled, lc_weight, fm_proj, fm_out, cotangent):
    t = lax.axis_index("x").astype(jnp.int32)[None]
    rep_count = lax.axis_size("zlo")
    sample_total = cotangent.shape[0] * rep_count * 32
    wide_scale = float(sample_total * 192) ** (-0.5)
    out_scale = float(sample_total * 256 * 192) ** (-0.5)
    rows = swap(pack_rows(t, pooled), TABLE)
    own = jnp.concatenate([lc_weight, fm_proj.T, fm_out], axis=1)
    weights = lax.all_gather(own, "x", axis=0, tiled=True)
    ig, igt, base, wt, p = upstream_terms(t, cotangent, weights)
    layer, messages = layer_terms(t, rows, cotangent, weights, ig, igt, base, wt, p)
    plane = plane_terms(swap(messages, PLANE))
    column = swap(plane, "zhi")
    layer_out = lax.all_gather(layer, "x", axis=0, tiled=True)
    column, _ = lax.optimization_barrier((column, layer_out))
    emb_grad, total = column_terms(column, rep_count)
    total = replica_terms(swap(total, "zlo"))
    lc_grad, proj_grad, out_grad = final_terms(swap(total, COLUMN), wide_scale, out_scale)
    return (layer_out, emb_grad.reshape(256, 8, 48), lc_grad, proj_grad.T, out_grad)


def solution(mesh):
    reps = mesh.shape["rep"]
    fine = Mesh(mesh.devices.reshape(reps, 4, 4, 2, 4), ("zlo", "zhi", "y", "core", "x"))
    in_specs = (
        P("zlo", TABLE, None),
        P("x", None),
        P(None, "x"),
        P("x", None),
        P(("zlo",) + TABLE, None, None),
    )
    out_specs = (
        P(("zlo",) + TABLE, None, None),
        P("zlo", TABLE, "x"),
        P("x", None),
        P(None, "x"),
        P("x", None),
    )
    return jax.shard_map(shards, mesh=fine, in_specs=in_specs, out_specs=out_specs, check_vma=False)
```

```python
import jax
import jax.numpy as jnp
from jax import lax
from jax.experimental import pallas as pl
from jax.experimental.pallas import tpu as pltpu
from jax.sharding import Mesh, PartitionSpec as P

BF = jnp.bfloat16
F32 = jnp.float32
TABLE = ("zhi", "y", "core")
PLANE = ("y", "core", "x")
COLUMN = ("y", "core")
TURN = 16
GROUP = [[(i + TURN) % 32 for i in range(32)]]
VMEM_BYTES = 48 * 1024 * 1024


def dot(a, b):
    return lax.dot_general(a, b, (((1,), (0,)), ((), ())), preferred_element_type=F32)


def dot_t(a, b):
    return lax.dot_general(a, b, (((1,), (1,)), ((), ())), preferred_element_type=F32)


def params():
    return pltpu.CompilerParams(vmem_limit_bytes=VMEM_BYTES)


def whole(shape):
    zeros = (0,) * len(shape)
    return pl.BlockSpec(shape, lambda i, t: zeros)


def pack_kernel(t_ref, pooled_ref, out_ref):
    first = pooled_ref[:, 0, 0].astype(F32)
    second = pooled_ref[:, 0, 1].astype(F32)
    n = first.shape[0]
    mixed = jnp.concatenate([first[:, :, 128:], second[:, :, 128:]], axis=2)
    rows = jnp.concatenate([first[:, :, :128], second[:, :, :128], mixed], axis=1)
    rows = rows.astype(BF)
    out_ref[0 : n - TURN] = rows[TURN:]
    out_ref[n - TURN :] = rows[:TURN]


def pack_rows(t, pooled):
    view = pooled.reshape(32, 4, 2, 8, 192)
    return pl.pallas_call(
        pack_kernel,
        grid_spec=pltpu.PrefetchScalarGridSpec(
            num_scalar_prefetch=1,
            grid=(1,),
            in_specs=[pl.BlockSpec((32, 1, 2, 8, 192), lambda i, t: (0, t[0], 0, 0, 0))],
            out_specs=whole((32, 24, 128)),
        ),
        out_shape=jax.ShapeDtypeStruct((32, 24, 128), BF),
        compiler_params=params(),
        name="pack_rows",
    )(t, view)


def upstream_kernel(t_ref, g_ref, w_ref, ig_ref, igt_ref, base_ref, wt_ref, p_ref):
    lc = w_ref[:, :256]
    pt = w_ref[:, 256:512]
    out_w = w_ref[:, 512:704]
    wt_ref[...] = lc.astype(F32).T.astype(BF)
    p_ref[...] = pt.astype(F32).T.astype(BF)
    for s in range(2):
        g = g_ref[s]
        ig_ref[s] = dot_t(g, out_w).astype(BF)
        igt_ref[s] = dot_t(out_w, g).astype(BF)
        base_ref[s] = g.astype(F32) + dot(lc, g)


def upstream_terms(t, cotangent, weights):
    return pl.pallas_call(
        upstream_kernel,
        grid_spec=pltpu.PrefetchScalarGridSpec(
            num_scalar_prefetch=1,
            grid=(1,),
            in_specs=[
                pl.BlockSpec((2, 256, 192), lambda i, t: (t[0], 0, 0)),
                whole((256, 704)),
            ],
            out_specs=[
                whole((2, 256, 256)),
                whole((2, 256, 256)),
                whole((2, 256, 192)),
                whole((256, 256)),
                whole((256, 256)),
            ],
        ),
        out_shape=[
            jax.ShapeDtypeStruct((2, 256, 256), BF),
            jax.ShapeDtypeStruct((2, 256, 256), BF),
            jax.ShapeDtypeStruct((2, 256, 192), F32),
            jax.ShapeDtypeStruct((256, 256), BF),
            jax.ShapeDtypeStruct((256, 256), BF),
        ],
        compiler_params=params(),
        name="upstream_terms",
    )(t, cotangent, weights)


def layer_kernel(t_ref, x_ref, g_ref, w_ref, ig_ref, igt_ref, base_ref, wt_ref, p_ref, layer_ref, msg_ref):
    pt = w_ref[:, 256:512]
    out_w = w_ref[:, 512:704]
    wt = wt_ref[...]
    planes = x_ref[...].astype(F32)
    planes = jnp.concatenate([planes[32 - TURN :], planes[: 32 - TURN]], axis=0)
    plane = [planes[:, 8 * i : 8 * i + 8].reshape(256, 128) for i in range(3)]
    xs = [
        jnp.concatenate([plane[0], plane[2][:, :64]], axis=1),
        jnp.concatenate([plane[1], plane[2][:, 64:]], axis=1),
    ]
    grads = []
    out_sum = proj_sum = lc_sum = None
    for s in range(2):
        x32 = xs[s]
        x = x32.astype(BF)
        g = g_ref[s]
        ct = dot(pt, x).astype(BF)
        inter = dot_t(x, ct).astype(BF)
        inter_t = dot_t(ct, x).astype(BF)
        forward = dot(inter, out_w) + dot(wt, x)
        layer_ref[s] = (x32 + forward).astype(BF)
        cgt = dot(igt_ref[s], x).astype(BF)
        grads.append(base_ref[s] + dot(ig_ref[s], ct) + dot(p_ref[...], cgt))
        out_term, proj_term, lc_term = dot(inter_t, g), dot_t(cgt, x), dot_t(x, g)
        out_sum = out_term if s == 0 else out_sum + out_term
        proj_sum = proj_term if s == 0 else proj_sum + proj_term
        lc_sum = lc_term if s == 0 else lc_sum + lc_term
    pad = jnp.zeros((256, 32), F32)
    emb = [
        jnp.concatenate([grads[0][:, 48 * q : 48 * q + 48], grads[1][:, 48 * q : 48 * q + 48], pad], axis=1)
        for q in range(4)
    ]
    out_tail = jnp.concatenate([out_sum[:, 128:], jnp.zeros((256, 64), F32)], axis=1)
    for c in range(8):
        for q in range(4):
            rows = slice(64 * q + 8 * c, 64 * q + 8 * c + 8)
            tiles = [emb[q][64 * z + 8 * c : 64 * z + 8 * c + 8] for z in range(4)]
            tiles += [lc_sum[rows, :128], lc_sum[rows, 128:]]
            tiles += [proj_sum[rows, :128], proj_sum[rows, 128:]]
            tiles += [out_sum[rows, :128], out_tail[rows]]
            msg_ref[4 * c + q] = jnp.concatenate(tiles, axis=0).astype(BF)


def layer_terms(t, rows, cotangent, weights, ig, igt, base, wt, p):
    return pl.pallas_call(
        layer_kernel,
        grid_spec=pltpu.PrefetchScalarGridSpec(
            num_scalar_prefetch=1,
            grid=(1,),
            in_specs=[
                whole((32, 24, 128)),
                pl.BlockSpec((2, 256, 192), lambda i, t: (t[0], 0, 0)),
                whole((256, 704)),
                whole((2, 256, 256)),
                whole((2, 256, 256)),
                whole((2, 256, 192)),
                whole((256, 256)),
                whole((256, 256)),
            ],
            out_specs=[whole((2, 256, 192)), whole((32, 80, 128))],
        ),
        out_shape=[
            jax.ShapeDtypeStruct((2, 256, 192), BF),
            jax.ShapeDtypeStruct((32, 80, 128), BF),
        ],
        compiler_params=params(),
        name="layer_terms",
    )(t, rows, cotangent, weights, ig, igt, base, wt, p)


def weight_kernel(in_ref, out_ref):
    total = in_ref[0, 32:80].astype(F32)
    for d in range(1, 32):
        total = total + in_ref[d, 32:80].astype(F32)
    total = total.astype(BF)
    for r in range(out_ref.shape[0]):
        out_ref[r] = total


def weight_terms(received, rep_count):
    return pl.pallas_call(
        weight_kernel,
        out_shape=jax.ShapeDtypeStruct((rep_count, 48, 128), BF),
        compiler_params=params(),
        name="weight_terms",
    )(received)


def plane_kernel(in_ref, out_ref):
    wide = []
    for c in range(8):
        parts = [in_ref[4 * c + q, 0:32].astype(F32)[:, :96] for q in range(4)]
        wide.append(jnp.concatenate(parts, axis=1))
    for z in range(4):
        rows = jnp.concatenate([wide[c][8 * z : 8 * z + 8] for c in range(8)], axis=0).astype(BF)
        for i in range(3):
            out_ref[z, 64 * i : 64 * i + 64] = rows[:, 128 * i : 128 * i + 128]


def plane_terms(received):
    return pl.pallas_call(
        plane_kernel,
        out_shape=jax.ShapeDtypeStruct((4, 192, 128), BF),
        compiler_params=params(),
        name="plane_terms",
    )(received)


def replica_kernel(weight_ref, emb_ref, out_ref):
    total = weight_ref[0].astype(F32)
    for r in range(1, weight_ref.shape[0]):
        total = total + weight_ref[r].astype(F32)
    total = total.astype(BF)
    for z in range(4):
        out_ref[z, 0:192] = emb_ref[z]
        out_ref[z, 192:240] = total


def replica_terms(weight, emb):
    return pl.pallas_call(
        replica_kernel,
        out_shape=jax.ShapeDtypeStruct((4, 240, 128), BF),
        compiler_params=params(),
        name="replica_terms",
    )(weight, emb)


def column_kernel(in_ref, emb_ref, total_ref):
    total = in_ref[0, 192:240].astype(F32)
    for z in range(1, 4):
        total = total + in_ref[z, 192:240].astype(F32)
    for c in range(8):
        total_ref[c] = total
    for z in range(4):
        planes = [in_ref[z, 64 * i : 64 * i + 64].astype(F32) for i in range(3)]
        rows = jnp.concatenate(planes, axis=1).reshape(8, 8, 384)
        for i in range(8):
            emb_ref[8 * z : 8 * z + 8, i] = rows[:, :, 48 * i : 48 * i + 48].astype(BF)


def column_terms(received):
    return pl.pallas_call(
        column_kernel,
        out_shape=[
            jax.ShapeDtypeStruct((32, 8, 8, 48), BF),
            jax.ShapeDtypeStruct((8, 48, 128), F32),
        ],
        compiler_params=params(),
        name="column_terms",
    )(received)


def copy_kernel(in_ref, out_ref):
    out_ref[...] = in_ref[...]


def settle(block):
    return pl.pallas_call(
        copy_kernel,
        out_shape=jax.ShapeDtypeStruct(block.shape, block.dtype),
        compiler_params=params(),
        name="settle",
    )(block)


def final_kernel(wide_scale, out_scale, in_ref, lc_ref, proj_ref, out_ref):
    rows = [in_ref[c] for c in range(8)]
    part = [jnp.concatenate([r[8 * i : 8 * i + 8] for r in rows], axis=0) for i in range(6)]
    lc_ref[...] = jnp.concatenate(part[0:2], axis=1) * wide_scale
    proj_ref[...] = jnp.concatenate(part[2:4], axis=1) * wide_scale
    out_ref[...] = jnp.concatenate([part[4], part[5][:, :64]], axis=1) * out_scale


def final_terms(received, wide_scale, out_scale):
    def kernel(*refs):
        final_kernel(wide_scale, out_scale, *refs)

    return pl.pallas_call(
        kernel,
        out_shape=[
            jax.ShapeDtypeStruct((64, 256), F32),
            jax.ShapeDtypeStruct((64, 256), F32),
            jax.ShapeDtypeStruct((64, 192), F32),
        ],
        compiler_params=params(),
        name="final_terms",
    )(received)


def swap(blocks, axes):
    return lax.all_to_all(blocks, axes, split_axis=0, concat_axis=0, tiled=True)


def shards(pooled, lc_weight, fm_proj, fm_out, cotangent):
    t = lax.axis_index("x").astype(jnp.int32)[None]
    rep_count = lax.axis_size("zlo")
    sample_total = cotangent.shape[0] * rep_count * 32
    wide_scale = float(sample_total * 192) ** (-0.5)
    out_scale = float(sample_total * 256 * 192) ** (-0.5)
    rows = lax.all_to_all(
        pack_rows(t, pooled), TABLE, split_axis=0, concat_axis=0, tiled=True, axis_index_groups=GROUP
    )
    own = jnp.concatenate([lc_weight, fm_proj.T, fm_out], axis=1)
    weights = lax.all_gather(own, "x", axis=0, tiled=True)
    ig, igt, base, wt, p = upstream_terms(t, cotangent, weights)
    layer, messages = layer_terms(t, rows, cotangent, weights, ig, igt, base, wt, p)
    received = swap(messages, PLANE)
    weight = swap(weight_terms(received, rep_count), "zlo")
    column = swap(replica_terms(weight, plane_terms(received)), "zhi")
    layer_out = settle(lax.all_gather(layer.transpose(0, 2, 1), "x", axis=0, tiled=True))
    column, _ = lax.optimization_barrier((column, layer_out))
    emb_grad, total = column_terms(column)
    lc_grad, proj_grad, out_grad = final_terms(swap(total, COLUMN), wide_scale, out_scale)
    return (layer_out.transpose(0, 2, 1), emb_grad.reshape(256, 8, 48), lc_grad, proj_grad.T, out_grad)


def solution(mesh):
    reps = mesh.shape["rep"]
    fine = Mesh(mesh.devices.reshape(reps, 4, 4, 2, 4), ("zlo", "zhi", "y", "core", "x"))
    in_specs = (
        P("zlo", TABLE, None),
        P("x", None),
        P(None, "x"),
        P("x", None),
        P(("zlo",) + TABLE, None, None),
    )
    out_specs = (
        P(("zlo",) + TABLE, None, None),
        P("zlo", TABLE, "x"),
        P("x", None),
        P(None, "x"),
        P("x", None),
    )
    return jax.shard_map(shards, mesh=fine, in_specs=in_specs, out_specs=out_specs, check_vma=False)
```

```python
import jax
import jax.numpy as jnp
from jax import lax
from jax.experimental import pallas as pl
from jax.experimental.pallas import tpu as pltpu
from jax.sharding import Mesh, PartitionSpec as P

BF = jnp.bfloat16
F32 = jnp.float32
TABLE = ("zhi", "y", "core")
PLANE = ("y", "core", "x")
COLUMN = ("y", "core")
TURN = 16
TABLE_ORDER = [(i + TURN) % 32 for i in range(32)]
COLUMN_ORDER = [2, 3, 0, 1]
VMEM_BYTES = 48 * 1024 * 1024


def dot(a, b):
    return lax.dot_general(a, b, (((1,), (0,)), ((), ())), preferred_element_type=F32)


def dot_t(a, b):
    return lax.dot_general(a, b, (((1,), (1,)), ((), ())), preferred_element_type=F32)


def params():
    return pltpu.CompilerParams(vmem_limit_bytes=VMEM_BYTES)


def whole(shape):
    zeros = (0,) * len(shape)
    return pl.BlockSpec(shape, lambda i, t: zeros)


def pack_kernel(t_ref, pooled_ref, out_ref):
    first = pooled_ref[:, 0, 0].astype(F32)
    second = pooled_ref[:, 0, 1].astype(F32)
    n = first.shape[0]
    mixed = jnp.concatenate([first[:, :, 128:], second[:, :, 128:]], axis=2)
    rows = jnp.concatenate([first[:, :, :128], second[:, :, :128], mixed], axis=1)
    rows = rows.astype(BF)
    out_ref[0 : n - TURN] = rows[TURN:]
    out_ref[n - TURN :] = rows[:TURN]


def pack_rows(t, pooled):
    view = pooled.reshape(32, 4, 2, 8, 192)
    return pl.pallas_call(
        pack_kernel,
        grid_spec=pltpu.PrefetchScalarGridSpec(
            num_scalar_prefetch=1,
            grid=(1,),
            in_specs=[pl.BlockSpec((32, 1, 2, 8, 192), lambda i, t: (0, t[0], 0, 0, 0))],
            out_specs=whole((32, 24, 128)),
        ),
        out_shape=jax.ShapeDtypeStruct((32, 24, 128), BF),
        compiler_params=params(),
        name="pack_rows",
    )(t, view)


def upstream_kernel(t_ref, g_ref, w_ref, ig_ref, igt_ref, base_ref, wt_ref, p_ref):
    lc = w_ref[:, :256]
    pt = w_ref[:, 256:512]
    out_w = w_ref[:, 512:704]
    wt_ref[...] = lc.astype(F32).T.astype(BF)
    p_ref[...] = pt.astype(F32).T.astype(BF)
    for s in range(2):
        g = g_ref[s]
        ig_ref[s] = dot_t(g, out_w).astype(BF)
        igt_ref[s] = dot_t(out_w, g).astype(BF)
        base_ref[s] = g.astype(F32) + dot(lc, g)


def upstream_terms(t, cotangent, weights):
    return pl.pallas_call(
        upstream_kernel,
        grid_spec=pltpu.PrefetchScalarGridSpec(
            num_scalar_prefetch=1,
            grid=(1,),
            in_specs=[
                pl.BlockSpec((2, 256, 192), lambda i, t: (t[0], 0, 0)),
                whole((256, 704)),
            ],
            out_specs=[
                whole((2, 256, 256)),
                whole((2, 256, 256)),
                whole((2, 256, 192)),
                whole((256, 256)),
                whole((256, 256)),
            ],
        ),
        out_shape=[
            jax.ShapeDtypeStruct((2, 256, 256), BF),
            jax.ShapeDtypeStruct((2, 256, 256), BF),
            jax.ShapeDtypeStruct((2, 256, 192), F32),
            jax.ShapeDtypeStruct((256, 256), BF),
            jax.ShapeDtypeStruct((256, 256), BF),
        ],
        compiler_params=params(),
        name="upstream_terms",
    )(t, cotangent, weights)


def layer_kernel(t_ref, x_ref, g_ref, w_ref, ig_ref, igt_ref, base_ref, wt_ref, p_ref, layer_ref, msg_ref):
    pt = w_ref[:, 256:512]
    out_w = w_ref[:, 512:704]
    wt = wt_ref[...]
    planes = x_ref[...].astype(F32)
    planes = jnp.concatenate([planes[32 - TURN :], planes[: 32 - TURN]], axis=0)
    plane = [planes[:, 8 * i : 8 * i + 8].reshape(256, 128) for i in range(3)]
    xs = [
        jnp.concatenate([plane[0], plane[2][:, :64]], axis=1),
        jnp.concatenate([plane[1], plane[2][:, 64:]], axis=1),
    ]
    grads = []
    out_sum = proj_sum = lc_sum = None
    for s in range(2):
        x32 = xs[s]
        x = x32.astype(BF)
        g = g_ref[s]
        ct = dot(pt, x).astype(BF)
        inter = dot_t(x, ct).astype(BF)
        inter_t = dot_t(ct, x).astype(BF)
        forward = dot(inter, out_w) + dot(wt, x)
        layer_ref[s] = (x32 + forward).astype(BF)
        cgt = dot(igt_ref[s], x).astype(BF)
        grads.append(base_ref[s] + dot(ig_ref[s], ct) + dot(p_ref[...], cgt))
        out_term, proj_term, lc_term = dot(inter_t, g), dot_t(cgt, x), dot_t(x, g)
        out_sum = out_term if s == 0 else out_sum + out_term
        proj_sum = proj_term if s == 0 else proj_sum + proj_term
        lc_sum = lc_term if s == 0 else lc_sum + lc_term
    pad = jnp.zeros((256, 32), F32)
    emb = [
        jnp.concatenate([grads[0][:, 48 * q : 48 * q + 48], grads[1][:, 48 * q : 48 * q + 48], pad], axis=1)
        for q in range(4)
    ]
    out_tail = jnp.concatenate([out_sum[:, 128:], jnp.zeros((256, 64), F32)], axis=1)
    for c in range(8):
        for q in range(4):
            rows = slice(64 * q + 8 * c, 64 * q + 8 * c + 8)
            tiles = [emb[q][64 * z + 8 * c : 64 * z + 8 * c + 8] for z in range(4)]
            tiles += [lc_sum[rows, :128], lc_sum[rows, 128:]]
            tiles += [proj_sum[rows, :128], proj_sum[rows, 128:]]
            tiles += [out_sum[rows, :128], out_tail[rows]]
            msg_ref[4 * c + q] = jnp.concatenate(tiles, axis=0).astype(BF)


def layer_terms(t, rows, cotangent, weights, ig, igt, base, wt, p):
    return pl.pallas_call(
        layer_kernel,
        grid_spec=pltpu.PrefetchScalarGridSpec(
            num_scalar_prefetch=1,
            grid=(1,),
            in_specs=[
                whole((32, 24, 128)),
                pl.BlockSpec((2, 256, 192), lambda i, t: (t[0], 0, 0)),
                whole((256, 704)),
                whole((2, 256, 256)),
                whole((2, 256, 256)),
                whole((2, 256, 192)),
                whole((256, 256)),
                whole((256, 256)),
            ],
            out_specs=[whole((2, 256, 192)), whole((32, 80, 128))],
        ),
        out_shape=[
            jax.ShapeDtypeStruct((2, 256, 192), BF),
            jax.ShapeDtypeStruct((32, 80, 128), BF),
        ],
        compiler_params=params(),
        name="layer_terms",
    )(t, rows, cotangent, weights, ig, igt, base, wt, p)


def weight_kernel(in_ref, out_ref):
    total = in_ref[0, 32:80].astype(F32)
    for d in range(1, 32):
        total = total + in_ref[d, 32:80].astype(F32)
    total = total.astype(BF)
    for r in range(out_ref.shape[0]):
        out_ref[r] = total


def weight_terms(received, rep_count):
    return pl.pallas_call(
        weight_kernel,
        out_shape=jax.ShapeDtypeStruct((rep_count, 48, 128), BF),
        compiler_params=params(),
        name="weight_terms",
    )(received)


def plane_kernel(in_ref, out_ref):
    wide = []
    for c in range(8):
        parts = [in_ref[4 * c + q, 0:32].astype(F32)[:, :96] for q in range(4)]
        wide.append(jnp.concatenate(parts, axis=1))
    for z in range(4):
        rows = jnp.concatenate([wide[c][8 * z : 8 * z + 8] for c in range(8)], axis=0).astype(BF)
        for i in range(3):
            out_ref[z, 64 * i : 64 * i + 64] = rows[:, 128 * i : 128 * i + 128]


def plane_terms(received):
    return pl.pallas_call(
        plane_kernel,
        out_shape=jax.ShapeDtypeStruct((4, 192, 128), BF),
        compiler_params=params(),
        name="plane_terms",
    )(received)


def replica_kernel(weight_ref, emb_ref, out_ref):
    total = weight_ref[0].astype(F32)
    for r in range(1, weight_ref.shape[0]):
        total = total + weight_ref[r].astype(F32)
    total = total.astype(BF)
    for z in range(4):
        out_ref[(z + 2) % 4, 0:192] = emb_ref[z]
        out_ref[z, 192:240] = total


def replica_terms(weight, emb):
    return pl.pallas_call(
        replica_kernel,
        out_shape=jax.ShapeDtypeStruct((4, 240, 128), BF),
        compiler_params=params(),
        name="replica_terms",
    )(weight, emb)


def total_kernel(in_ref, out_ref):
    total = in_ref[0, 192:240].astype(F32)
    for z in range(1, 4):
        total = total + in_ref[z, 192:240].astype(F32)
    total = total.astype(BF)
    for c in range(8):
        out_ref[c] = total


def total_terms(received):
    return pl.pallas_call(
        total_kernel,
        out_shape=jax.ShapeDtypeStruct((8, 48, 128), BF),
        compiler_params=params(),
        name="total_terms",
    )(received)


def column_kernel(in_ref, emb_ref):
    for z in range(4):
        planes = [in_ref[(z + 2) % 4, 64 * i : 64 * i + 64].astype(F32) for i in range(3)]
        rows = jnp.concatenate(planes, axis=1).reshape(8, 8, 384)
        for i in range(8):
            emb_ref[8 * z : 8 * z + 8, i] = rows[:, :, 48 * i : 48 * i + 48].astype(BF)


def column_terms(received):
    return pl.pallas_call(
        column_kernel,
        out_shape=jax.ShapeDtypeStruct((32, 8, 8, 48), BF),
        compiler_params=params(),
        name="column_terms",
    )(received)


def copy_kernel(in_ref, out_ref):
    out_ref[...] = in_ref[...]


def settle(block):
    return pl.pallas_call(
        copy_kernel,
        out_shape=jax.ShapeDtypeStruct(block.shape, block.dtype),
        compiler_params=params(),
        name="settle",
    )(block)


def final_kernel(wide_scale, out_scale, in_ref, lc_ref, proj_ref, out_ref):
    rows = [in_ref[c].astype(F32) for c in range(8)]
    part = [jnp.concatenate([r[8 * i : 8 * i + 8] for r in rows], axis=0) for i in range(6)]
    lc_ref[...] = jnp.concatenate(part[0:2], axis=1) * wide_scale
    proj_ref[...] = jnp.concatenate(part[2:4], axis=1) * wide_scale
    out_ref[...] = jnp.concatenate([part[4], part[5][:, :64]], axis=1) * out_scale


def final_terms(received, wide_scale, out_scale):
    def kernel(*refs):
        final_kernel(wide_scale, out_scale, *refs)

    return pl.pallas_call(
        kernel,
        out_shape=[
            jax.ShapeDtypeStruct((64, 256), F32),
            jax.ShapeDtypeStruct((64, 256), F32),
            jax.ShapeDtypeStruct((64, 192), F32),
        ],
        compiler_params=params(),
        name="final_terms",
    )(received)


def swap(blocks, axes, order=None):
    groups = None if order is None else [order]
    return lax.all_to_all(blocks, axes, split_axis=0, concat_axis=0, tiled=True, axis_index_groups=groups)


def shards(pooled, lc_weight, fm_proj, fm_out, cotangent):
    t = lax.axis_index("x").astype(jnp.int32)[None]
    rep_count = lax.axis_size("zlo")
    sample_total = cotangent.shape[0] * rep_count * 32
    wide_scale = float(sample_total * 192) ** (-0.5)
    out_scale = float(sample_total * 256 * 192) ** (-0.5)
    middle_first = sorted(range(rep_count), key=lambda r: abs(2 * r - rep_count))
    rows = swap(pack_rows(t, pooled), TABLE, TABLE_ORDER)
    own = jnp.concatenate([lc_weight, fm_proj.T, fm_out], axis=1)
    weights = lax.all_gather(own, "x", axis=0, tiled=True)
    ig, igt, base, wt, p = upstream_terms(t, cotangent, weights)
    layer, messages = layer_terms(t, rows, cotangent, weights, ig, igt, base, wt, p)
    received = swap(messages, PLANE)
    weight = swap(weight_terms(received, rep_count), "zlo", middle_first)
    column = swap(replica_terms(weight, plane_terms(received)), "zhi", COLUMN_ORDER)
    layer_out = settle(lax.all_gather(layer.transpose(0, 2, 1), "x", axis=0, tiled=True))
    column, _ = lax.optimization_barrier((column, layer_out))
    total = swap(total_terms(column), COLUMN)
    emb_grad = column_terms(column)
    lc_grad, proj_grad, out_grad = final_terms(total, wide_scale, out_scale)
    return (layer_out.transpose(0, 2, 1), emb_grad.reshape(256, 8, 48), lc_grad, proj_grad.T, out_grad)


def solution(mesh):
    reps = mesh.shape["rep"]
    fine = Mesh(mesh.devices.reshape(reps, 4, 4, 2, 4), ("zlo", "zhi", "y", "core", "x"))
    in_specs = (
        P("zlo", TABLE, None),
        P("x", None),
        P(None, "x"),
        P("x", None),
        P(("zlo",) + TABLE, None, None),
    )
    out_specs = (
        P(("zlo",) + TABLE, None, None),
        P("zlo", TABLE, "x"),
        P("x", None),
        P(None, "x"),
        P("x", None),
    )
    return jax.shard_map(shards, mesh=fine, in_specs=in_specs, out_specs=out_specs, check_vma=False)
```

```python
import jax
import jax.numpy as jnp
from jax import lax
from jax.experimental import pallas as pl
from jax.experimental.pallas import tpu as pltpu
from jax.sharding import Mesh, PartitionSpec as P

BF = jnp.bfloat16
F32 = jnp.float32
TABLE = ("zhi", "y", "core")
PLANE = ("y", "core", "x")
COLUMN = ("y", "core")
COLUMN_ORDER = [2, 3, 0, 1]
FAR_FIRST = [5, 4, 7, 6, 1, 0, 3, 2]
TABLE_ORDER = [8 * z + c for z in COLUMN_ORDER for c in FAR_FIRST]
VMEM_BYTES = 48 * 1024 * 1024


def dot(a, b):
    return lax.dot_general(a, b, (((1,), (0,)), ((), ())), preferred_element_type=F32)


def dot_t(a, b):
    return lax.dot_general(a, b, (((1,), (1,)), ((), ())), preferred_element_type=F32)


def params():
    return pltpu.CompilerParams(vmem_limit_bytes=VMEM_BYTES)


def whole(shape):
    zeros = (0,) * len(shape)
    return pl.BlockSpec(shape, lambda i, t: zeros)


def pack_kernel(t_ref, pooled_ref, out_ref):
    first = pooled_ref[:, 0, 0].astype(F32)
    second = pooled_ref[:, 0, 1].astype(F32)
    mixed = jnp.concatenate([first[:, :, 128:], second[:, :, 128:]], axis=2)
    rows = jnp.concatenate([first[:, :, :128], second[:, :, :128], mixed], axis=1)
    rows = rows.astype(BF)
    for k, d in enumerate(TABLE_ORDER):
        out_ref[k] = rows[d]


def pack_rows(t, pooled):
    view = pooled.reshape(32, 4, 2, 8, 192)
    return pl.pallas_call(
        pack_kernel,
        grid_spec=pltpu.PrefetchScalarGridSpec(
            num_scalar_prefetch=1,
            grid=(1,),
            in_specs=[pl.BlockSpec((32, 1, 2, 8, 192), lambda i, t: (0, t[0], 0, 0, 0))],
            out_specs=whole((32, 24, 128)),
        ),
        out_shape=jax.ShapeDtypeStruct((32, 24, 128), BF),
        compiler_params=params(),
        name="pack_rows",
    )(t, view)


def upstream_kernel(t_ref, g_ref, w_ref, ig_ref, igt_ref, base_ref, wt_ref, p_ref):
    lc = w_ref[:, :256]
    pt = w_ref[:, 256:512]
    out_w = w_ref[:, 512:704]
    wt_ref[...] = lc.astype(F32).T.astype(BF)
    p_ref[...] = pt.astype(F32).T.astype(BF)
    for s in range(2):
        g = g_ref[s]
        ig_ref[s] = dot_t(g, out_w).astype(BF)
        igt_ref[s] = dot_t(out_w, g).astype(BF)
        base_ref[s] = g.astype(F32) + dot(lc, g)


def upstream_terms(t, cotangent, weights):
    return pl.pallas_call(
        upstream_kernel,
        grid_spec=pltpu.PrefetchScalarGridSpec(
            num_scalar_prefetch=1,
            grid=(1,),
            in_specs=[
                pl.BlockSpec((2, 256, 192), lambda i, t: (t[0], 0, 0)),
                whole((256, 704)),
            ],
            out_specs=[
                whole((2, 256, 256)),
                whole((2, 256, 256)),
                whole((2, 256, 192)),
                whole((256, 256)),
                whole((256, 256)),
            ],
        ),
        out_shape=[
            jax.ShapeDtypeStruct((2, 256, 256), BF),
            jax.ShapeDtypeStruct((2, 256, 256), BF),
            jax.ShapeDtypeStruct((2, 256, 192), F32),
            jax.ShapeDtypeStruct((256, 256), BF),
            jax.ShapeDtypeStruct((256, 256), BF),
        ],
        compiler_params=params(),
        name="upstream_terms",
    )(t, cotangent, weights)


def layer_kernel(t_ref, x_ref, g_ref, w_ref, ig_ref, igt_ref, base_ref, wt_ref, p_ref, layer_ref, msg_ref):
    pt = w_ref[:, 256:512]
    out_w = w_ref[:, 512:704]
    wt = wt_ref[...]
    planes = x_ref[...].astype(F32)
    planes = jnp.stack([planes[TABLE_ORDER.index(d)] for d in range(32)], axis=0)
    plane = [planes[:, 8 * i : 8 * i + 8].reshape(256, 128) for i in range(3)]
    xs = [
        jnp.concatenate([plane[0], plane[2][:, :64]], axis=1),
        jnp.concatenate([plane[1], plane[2][:, 64:]], axis=1),
    ]
    grads = []
    out_sum = proj_sum = lc_sum = None
    for s in range(2):
        x32 = xs[s]
        x = x32.astype(BF)
        g = g_ref[s]
        ct = dot(pt, x).astype(BF)
        inter = dot_t(x, ct).astype(BF)
        inter_t = dot_t(ct, x).astype(BF)
        forward = dot(inter, out_w) + dot(wt, x)
        layer_ref[s] = (x32 + forward).astype(BF)
        cgt = dot(igt_ref[s], x).astype(BF)
        grads.append(base_ref[s] + dot(ig_ref[s], ct) + dot(p_ref[...], cgt))
        out_term, proj_term, lc_term = dot(inter_t, g), dot_t(cgt, x), dot_t(x, g)
        out_sum = out_term if s == 0 else out_sum + out_term
        proj_sum = proj_term if s == 0 else proj_sum + proj_term
        lc_sum = lc_term if s == 0 else lc_sum + lc_term
    pad = jnp.zeros((256, 32), F32)
    emb = [
        jnp.concatenate([grads[0][:, 48 * q : 48 * q + 48], grads[1][:, 48 * q : 48 * q + 48], pad], axis=1)
        for q in range(4)
    ]
    out_tail = jnp.concatenate([out_sum[:, 128:], jnp.zeros((256, 64), F32)], axis=1)
    for c in range(8):
        for q in range(4):
            rows = slice(64 * q + 8 * c, 64 * q + 8 * c + 8)
            tiles = [emb[q][64 * z + 8 * c : 64 * z + 8 * c + 8] for z in range(4)]
            tiles += [lc_sum[rows, :128], lc_sum[rows, 128:]]
            tiles += [proj_sum[rows, :128], proj_sum[rows, 128:]]
            tiles += [out_sum[rows, :128], out_tail[rows]]
            msg_ref[4 * c + q] = jnp.concatenate(tiles, axis=0).astype(BF)


def layer_terms(t, rows, cotangent, weights, ig, igt, base, wt, p):
    return pl.pallas_call(
        layer_kernel,
        grid_spec=pltpu.PrefetchScalarGridSpec(
            num_scalar_prefetch=1,
            grid=(1,),
            in_specs=[
                whole((32, 24, 128)),
                pl.BlockSpec((2, 256, 192), lambda i, t: (t[0], 0, 0)),
                whole((256, 704)),
                whole((2, 256, 256)),
                whole((2, 256, 256)),
                whole((2, 256, 192)),
                whole((256, 256)),
                whole((256, 256)),
            ],
            out_specs=[whole((2, 256, 192)), whole((32, 80, 128))],
        ),
        out_shape=[
            jax.ShapeDtypeStruct((2, 256, 192), BF),
            jax.ShapeDtypeStruct((32, 80, 128), BF),
        ],
        compiler_params=params(),
        name="layer_terms",
    )(t, rows, cotangent, weights, ig, igt, base, wt, p)


def weight_kernel(in_ref, out_ref):
    total = in_ref[0, 32:80].astype(F32)
    for d in range(1, 32):
        total = total + in_ref[d, 32:80].astype(F32)
    total = total.astype(BF)
    for r in range(out_ref.shape[0]):
        out_ref[r] = total


def weight_terms(received, rep_count):
    return pl.pallas_call(
        weight_kernel,
        out_shape=jax.ShapeDtypeStruct((rep_count, 48, 128), BF),
        compiler_params=params(),
        name="weight_terms",
    )(received)


def plane_kernel(in_ref, out_ref):
    wide = []
    for c in range(8):
        parts = [in_ref[4 * c + q, 0:32].astype(F32)[:, :96] for q in range(4)]
        wide.append(jnp.concatenate(parts, axis=1))
    for z in range(4):
        rows = jnp.concatenate([wide[c][8 * z : 8 * z + 8] for c in range(8)], axis=0).astype(BF)
        for i in range(3):
            out_ref[z, 64 * i : 64 * i + 64] = rows[:, 128 * i : 128 * i + 128]


def plane_terms(received):
    return pl.pallas_call(
        plane_kernel,
        out_shape=jax.ShapeDtypeStruct((4, 192, 128), BF),
        compiler_params=params(),
        name="plane_terms",
    )(received)


def replica_kernel(weight_ref, emb_ref, out_ref):
    total = weight_ref[0].astype(F32)
    for r in range(1, weight_ref.shape[0]):
        total = total + weight_ref[r].astype(F32)
    total = total.astype(BF)
    for z in range(4):
        out_ref[COLUMN_ORDER.index(z), 0:192] = emb_ref[z]
        out_ref[z, 192:240] = total


def replica_terms(weight, emb):
    return pl.pallas_call(
        replica_kernel,
        out_shape=jax.ShapeDtypeStruct((4, 240, 128), BF),
        compiler_params=params(),
        name="replica_terms",
    )(weight, emb)


def total_kernel(in_ref, out_ref):
    total = in_ref[0, 192:240].astype(F32)
    for z in range(1, 4):
        total = total + in_ref[z, 192:240].astype(F32)
    total = total.astype(BF)
    for c in range(8):
        out_ref[c] = total


def total_terms(received):
    return pl.pallas_call(
        total_kernel,
        out_shape=jax.ShapeDtypeStruct((8, 48, 128), BF),
        compiler_params=params(),
        name="total_terms",
    )(received)


def column_kernel(in_ref, emb_ref):
    for z in range(4):
        planes = [in_ref[COLUMN_ORDER.index(z), 64 * i : 64 * i + 64].astype(F32) for i in range(3)]
        rows = jnp.concatenate(planes, axis=1).reshape(8, 8, 384)
        for i in range(8):
            emb_ref[8 * z : 8 * z + 8, i] = rows[:, :, 48 * i : 48 * i + 48].astype(BF)


def column_terms(received):
    return pl.pallas_call(
        column_kernel,
        out_shape=jax.ShapeDtypeStruct((32, 8, 8, 48), BF),
        compiler_params=params(),
        name="column_terms",
    )(received)


def copy_kernel(in_ref, out_ref):
    out_ref[...] = in_ref[...]


def settle(block):
    return pl.pallas_call(
        copy_kernel,
        out_shape=jax.ShapeDtypeStruct(block.shape, block.dtype),
        compiler_params=params(),
        name="settle",
    )(block)


def final_kernel(wide_scale, out_scale, in_ref, lc_ref, proj_ref, out_ref):
    rows = [in_ref[FAR_FIRST.index(c)].astype(F32) for c in range(8)]
    part = [jnp.concatenate([r[8 * i : 8 * i + 8] for r in rows], axis=0) for i in range(6)]
    lc_ref[...] = jnp.concatenate(part[0:2], axis=1) * wide_scale
    proj_ref[...] = jnp.concatenate(part[2:4], axis=1) * wide_scale
    out_ref[...] = jnp.concatenate([part[4], part[5][:, :64]], axis=1) * out_scale


def final_terms(received, wide_scale, out_scale):
    def kernel(*refs):
        final_kernel(wide_scale, out_scale, *refs)

    return pl.pallas_call(
        kernel,
        out_shape=[
            jax.ShapeDtypeStruct((64, 256), F32),
            jax.ShapeDtypeStruct((64, 256), F32),
            jax.ShapeDtypeStruct((64, 192), F32),
        ],
        compiler_params=params(),
        name="final_terms",
    )(received)


def swap(blocks, axes, order=None):
    groups = None if order is None else [order]
    return lax.all_to_all(blocks, axes, split_axis=0, concat_axis=0, tiled=True, axis_index_groups=groups)


def shards(pooled, lc_weight, fm_proj, fm_out, cotangent):
    t = lax.axis_index("x").astype(jnp.int32)[None]
    rep_count = lax.axis_size("zlo")
    sample_total = cotangent.shape[0] * rep_count * 32
    wide_scale = float(sample_total * 192) ** (-0.5)
    out_scale = float(sample_total * 256 * 192) ** (-0.5)
    middle_first = sorted(range(rep_count), key=lambda r: abs(2 * r - rep_count))
    rows = swap(pack_rows(t, pooled), TABLE, TABLE_ORDER)
    own = jnp.concatenate([lc_weight, fm_proj.T, fm_out], axis=1)
    weights = lax.all_gather(own, "x", axis=0, tiled=True)
    ig, igt, base, wt, p = upstream_terms(t, cotangent, weights)
    layer, messages = layer_terms(t, rows, cotangent, weights, ig, igt, base, wt, p)
    received = swap(messages, PLANE)
    weight = swap(weight_terms(received, rep_count), "zlo", middle_first)
    column = swap(replica_terms(weight, plane_terms(received)), "zhi", COLUMN_ORDER)
    layer_out = settle(lax.all_gather(layer.transpose(0, 2, 1), "x", axis=0, tiled=True))
    column, _ = lax.optimization_barrier((column, layer_out))
    total = swap(total_terms(column), COLUMN, FAR_FIRST)
    emb_grad = column_terms(column)
    lc_grad, proj_grad, out_grad = final_terms(total, wide_scale, out_scale)
    return (layer_out.transpose(0, 2, 1), emb_grad.reshape(256, 8, 48), lc_grad, proj_grad.T, out_grad)


def solution(mesh):
    reps = mesh.shape["rep"]
    fine = Mesh(mesh.devices.reshape(reps, 4, 4, 2, 4), ("zlo", "zhi", "y", "core", "x"))
    in_specs = (
        P("zlo", TABLE, None),
        P("x", None),
        P(None, "x"),
        P("x", None),
        P(("zlo",) + TABLE, None, None),
    )
    out_specs = (
        P(("zlo",) + TABLE, None, None),
        P("zlo", TABLE, "x"),
        P("x", None),
        P(None, "x"),
        P("x", None),
    )
    return jax.shard_map(shards, mesh=fine, in_specs=in_specs, out_specs=out_specs, check_vma=False)
```

```python
import jax
import jax.numpy as jnp
from jax import lax
from jax.experimental import pallas as pl
from jax.experimental.pallas import tpu as pltpu
from jax.sharding import Mesh, PartitionSpec as P

BF = jnp.bfloat16
F32 = jnp.float32
TABLE = ("zhi", "y", "core")
PLANE = ("y", "core", "x")
COLUMN = ("y", "core")
COLUMN_ORDER = [2, 3, 0, 1]
FAR_FIRST = [5, 4, 7, 6, 1, 0, 3, 2]
TABLE_ORDER = [8 * z + c for z in COLUMN_ORDER for c in FAR_FIRST]
PLANE_ORDER = [4 * c + q for c in FAR_FIRST for q in (2, 3, 0, 1)]
VMEM_BYTES = 48 * 1024 * 1024


def dot(a, b):
    return lax.dot_general(a, b, (((1,), (0,)), ((), ())), preferred_element_type=F32)


def dot_t(a, b):
    return lax.dot_general(a, b, (((1,), (1,)), ((), ())), preferred_element_type=F32)


def params():
    return pltpu.CompilerParams(vmem_limit_bytes=VMEM_BYTES)


def whole(shape):
    zeros = (0,) * len(shape)
    return pl.BlockSpec(shape, lambda i, t: zeros)


def pack_kernel(t_ref, pooled_ref, out_ref):
    first = pooled_ref[:, 0, 0].astype(F32)
    second = pooled_ref[:, 0, 1].astype(F32)
    mixed = jnp.concatenate([first[:, :, 128:], second[:, :, 128:]], axis=2)
    rows = jnp.concatenate([first[:, :, :128], second[:, :, :128], mixed], axis=1)
    rows = rows.astype(BF)
    for k, d in enumerate(TABLE_ORDER):
        out_ref[k] = rows[d]


def pack_rows(t, pooled):
    view = pooled.reshape(32, 4, 2, 8, 192)
    return pl.pallas_call(
        pack_kernel,
        grid_spec=pltpu.PrefetchScalarGridSpec(
            num_scalar_prefetch=1,
            grid=(1,),
            in_specs=[pl.BlockSpec((32, 1, 2, 8, 192), lambda i, t: (0, t[0], 0, 0, 0))],
            out_specs=whole((32, 24, 128)),
        ),
        out_shape=jax.ShapeDtypeStruct((32, 24, 128), BF),
        compiler_params=params(),
        name="pack_rows",
    )(t, view)


def upstream_kernel(t_ref, g_ref, w_ref, ig_ref, igt_ref, base_ref, wt_ref, p_ref):
    lc = w_ref[:, :256]
    pt = w_ref[:, 256:512]
    out_w = w_ref[:, 512:704]
    wt_ref[...] = lc.astype(F32).T.astype(BF)
    p_ref[...] = pt.astype(F32).T.astype(BF)
    for s in range(2):
        g = g_ref[s]
        ig_ref[s] = dot_t(g, out_w).astype(BF)
        igt_ref[s] = dot_t(out_w, g).astype(BF)
        base_ref[s] = g.astype(F32) + dot(lc, g)


def upstream_terms(t, cotangent, weights):
    return pl.pallas_call(
        upstream_kernel,
        grid_spec=pltpu.PrefetchScalarGridSpec(
            num_scalar_prefetch=1,
            grid=(1,),
            in_specs=[
                pl.BlockSpec((2, 256, 192), lambda i, t: (t[0], 0, 0)),
                whole((256, 704)),
            ],
            out_specs=[
                whole((2, 256, 256)),
                whole((2, 256, 256)),
                whole((2, 256, 192)),
                whole((256, 256)),
                whole((256, 256)),
            ],
        ),
        out_shape=[
            jax.ShapeDtypeStruct((2, 256, 256), BF),
            jax.ShapeDtypeStruct((2, 256, 256), BF),
            jax.ShapeDtypeStruct((2, 256, 192), F32),
            jax.ShapeDtypeStruct((256, 256), BF),
            jax.ShapeDtypeStruct((256, 256), BF),
        ],
        compiler_params=params(),
        name="upstream_terms",
    )(t, cotangent, weights)


def layer_kernel(t_ref, x_ref, g_ref, w_ref, ig_ref, igt_ref, base_ref, wt_ref, p_ref, layer_ref, msg_ref):
    pt = w_ref[:, 256:512]
    out_w = w_ref[:, 512:704]
    wt = wt_ref[...]
    planes = x_ref[...].astype(F32)
    planes = jnp.stack([planes[TABLE_ORDER.index(d)] for d in range(32)], axis=0)
    plane = [planes[:, 8 * i : 8 * i + 8].reshape(256, 128) for i in range(3)]
    xs = [
        jnp.concatenate([plane[0], plane[2][:, :64]], axis=1),
        jnp.concatenate([plane[1], plane[2][:, 64:]], axis=1),
    ]
    grads = []
    out_sum = proj_sum = lc_sum = None
    for s in range(2):
        x32 = xs[s]
        x = x32.astype(BF)
        g = g_ref[s]
        ct = dot(pt, x).astype(BF)
        inter = dot_t(x, ct).astype(BF)
        inter_t = dot_t(ct, x).astype(BF)
        forward = dot(inter, out_w) + dot(wt, x)
        layer_ref[s] = (x32 + forward).astype(BF)
        cgt = dot(igt_ref[s], x).astype(BF)
        grads.append(base_ref[s] + dot(ig_ref[s], ct) + dot(p_ref[...], cgt))
        out_term, proj_term, lc_term = dot(inter_t, g), dot_t(cgt, x), dot_t(x, g)
        out_sum = out_term if s == 0 else out_sum + out_term
        proj_sum = proj_term if s == 0 else proj_sum + proj_term
        lc_sum = lc_term if s == 0 else lc_sum + lc_term
    pad = jnp.zeros((256, 32), F32)
    emb = [
        jnp.concatenate([grads[0][:, 48 * q : 48 * q + 48], grads[1][:, 48 * q : 48 * q + 48], pad], axis=1)
        for q in range(4)
    ]
    out_tail = jnp.concatenate([out_sum[:, 128:], jnp.zeros((256, 64), F32)], axis=1)
    for c in range(8):
        for q in range(4):
            rows = slice(64 * q + 8 * c, 64 * q + 8 * c + 8)
            tiles = [emb[q][64 * z + 8 * c : 64 * z + 8 * c + 8] for z in range(4)]
            tiles += [lc_sum[rows, :128], lc_sum[rows, 128:]]
            tiles += [proj_sum[rows, :128], proj_sum[rows, 128:]]
            tiles += [out_sum[rows, :128], out_tail[rows]]
            msg_ref[PLANE_ORDER.index(4 * c + q)] = jnp.concatenate(tiles, axis=0).astype(BF)


def layer_terms(t, rows, cotangent, weights, ig, igt, base, wt, p):
    return pl.pallas_call(
        layer_kernel,
        grid_spec=pltpu.PrefetchScalarGridSpec(
            num_scalar_prefetch=1,
            grid=(1,),
            in_specs=[
                whole((32, 24, 128)),
                pl.BlockSpec((2, 256, 192), lambda i, t: (t[0], 0, 0)),
                whole((256, 704)),
                whole((2, 256, 256)),
                whole((2, 256, 256)),
                whole((2, 256, 192)),
                whole((256, 256)),
                whole((256, 256)),
            ],
            out_specs=[whole((2, 256, 192)), whole((32, 80, 128))],
        ),
        out_shape=[
            jax.ShapeDtypeStruct((2, 256, 192), BF),
            jax.ShapeDtypeStruct((32, 80, 128), BF),
        ],
        compiler_params=params(),
        name="layer_terms",
    )(t, rows, cotangent, weights, ig, igt, base, wt, p)


def weight_kernel(in_ref, out_ref):
    total = in_ref[0, 32:80].astype(F32)
    for d in range(1, 32):
        total = total + in_ref[d, 32:80].astype(F32)
    total = total.astype(BF)
    for r in range(out_ref.shape[0]):
        out_ref[r] = total


def weight_terms(received, rep_count):
    return pl.pallas_call(
        weight_kernel,
        out_shape=jax.ShapeDtypeStruct((rep_count, 48, 128), BF),
        compiler_params=params(),
        name="weight_terms",
    )(received)


def plane_kernel(in_ref, out_ref):
    wide = []
    for c in range(8):
        parts = [in_ref[PLANE_ORDER.index(4 * c + q), 0:32].astype(F32)[:, :96] for q in range(4)]
        wide.append(jnp.concatenate(parts, axis=1))
    for z in range(4):
        rows = jnp.concatenate([wide[c][8 * z : 8 * z + 8] for c in range(8)], axis=0).astype(BF)
        for i in range(3):
            out_ref[z, 64 * i : 64 * i + 64] = rows[:, 128 * i : 128 * i + 128]


def plane_terms(received):
    return pl.pallas_call(
        plane_kernel,
        out_shape=jax.ShapeDtypeStruct((4, 192, 128), BF),
        compiler_params=params(),
        name="plane_terms",
    )(received)


def replica_kernel(weight_ref, emb_ref, out_ref):
    total = weight_ref[0].astype(F32)
    for r in range(1, weight_ref.shape[0]):
        total = total + weight_ref[r].astype(F32)
    total = total.astype(BF)
    for z in range(4):
        out_ref[COLUMN_ORDER.index(z), 0:192] = emb_ref[z]
        out_ref[z, 192:240] = total


def replica_terms(weight, emb):
    return pl.pallas_call(
        replica_kernel,
        out_shape=jax.ShapeDtypeStruct((4, 240, 128), BF),
        compiler_params=params(),
        name="replica_terms",
    )(weight, emb)


def total_kernel(in_ref, out_ref):
    total = in_ref[0, 192:240].astype(F32)
    for z in range(1, 4):
        total = total + in_ref[z, 192:240].astype(F32)
    total = total.astype(BF)
    for c in range(8):
        out_ref[c] = total


def total_terms(received):
    return pl.pallas_call(
        total_kernel,
        out_shape=jax.ShapeDtypeStruct((8, 48, 128), BF),
        compiler_params=params(),
        name="total_terms",
    )(received)


def column_kernel(in_ref, emb_ref):
    for z in range(4):
        planes = [in_ref[COLUMN_ORDER.index(z), 64 * i : 64 * i + 64].astype(F32) for i in range(3)]
        rows = jnp.concatenate(planes, axis=1).reshape(8, 8, 384)
        for i in range(8):
            emb_ref[8 * z : 8 * z + 8, i] = rows[:, :, 48 * i : 48 * i + 48].astype(BF)


def column_terms(received):
    return pl.pallas_call(
        column_kernel,
        out_shape=jax.ShapeDtypeStruct((32, 8, 8, 48), BF),
        compiler_params=params(),
        name="column_terms",
    )(received)


def copy_kernel(in_ref, out_ref):
    out_ref[...] = in_ref[...]


def settle(block):
    return pl.pallas_call(
        copy_kernel,
        out_shape=jax.ShapeDtypeStruct(block.shape, block.dtype),
        compiler_params=params(),
        name="settle",
    )(block)


def final_kernel(wide_scale, out_scale, in_ref, lc_ref, proj_ref, out_ref):
    rows = [in_ref[FAR_FIRST.index(c)].astype(F32) for c in range(8)]
    part = [jnp.concatenate([r[8 * i : 8 * i + 8] for r in rows], axis=0) for i in range(6)]
    lc_ref[...] = jnp.concatenate(part[0:2], axis=1) * wide_scale
    proj_ref[...] = jnp.concatenate(part[2:4], axis=1) * wide_scale
    out_ref[...] = jnp.concatenate([part[4], part[5][:, :64]], axis=1) * out_scale


def final_terms(received, wide_scale, out_scale):
    def kernel(*refs):
        final_kernel(wide_scale, out_scale, *refs)

    return pl.pallas_call(
        kernel,
        out_shape=[
            jax.ShapeDtypeStruct((64, 256), F32),
            jax.ShapeDtypeStruct((64, 256), F32),
            jax.ShapeDtypeStruct((64, 192), F32),
        ],
        compiler_params=params(),
        name="final_terms",
    )(received)


def swap(blocks, axes, order=None):
    groups = None if order is None else [order]
    return lax.all_to_all(blocks, axes, split_axis=0, concat_axis=0, tiled=True, axis_index_groups=groups)


def shards(pooled, lc_weight, fm_proj, fm_out, cotangent):
    t = lax.axis_index("x").astype(jnp.int32)[None]
    rep_count = lax.axis_size("zlo")
    sample_total = cotangent.shape[0] * rep_count * 32
    wide_scale = float(sample_total * 192) ** (-0.5)
    out_scale = float(sample_total * 256 * 192) ** (-0.5)
    middle_first = sorted(range(rep_count), key=lambda r: abs(2 * r - rep_count))
    rows = swap(pack_rows(t, pooled), TABLE, TABLE_ORDER)
    own = jnp.concatenate([lc_weight, fm_proj.T, fm_out], axis=1)
    weights = lax.all_gather(own, "x", axis=0, tiled=True)
    ig, igt, base, wt, p = upstream_terms(t, cotangent, weights)
    layer, messages = layer_terms(t, rows, cotangent, weights, ig, igt, base, wt, p)
    received = swap(messages, PLANE, PLANE_ORDER)
    weight = swap(weight_terms(received, rep_count), "zlo", middle_first)
    column = swap(replica_terms(weight, plane_terms(received)), "zhi", COLUMN_ORDER)
    layer_out = settle(lax.all_gather(layer.transpose(0, 2, 1), "x", axis=0, tiled=True))
    column, _ = lax.optimization_barrier((column, layer_out))
    total = swap(total_terms(column), COLUMN, FAR_FIRST)
    emb_grad = column_terms(column)
    lc_grad, proj_grad, out_grad = final_terms(total, wide_scale, out_scale)
    return (layer_out.transpose(0, 2, 1), emb_grad.reshape(256, 8, 48), lc_grad, proj_grad.T, out_grad)


def solution(mesh):
    reps = mesh.shape["rep"]
    fine = Mesh(mesh.devices.reshape(reps, 4, 4, 2, 4), ("zlo", "zhi", "y", "core", "x"))
    in_specs = (
        P("zlo", TABLE, None),
        P("x", None),
        P(None, "x"),
        P("x", None),
        P(("zlo",) + TABLE, None, None),
    )
    out_specs = (
        P(("zlo",) + TABLE, None, None),
        P("zlo", TABLE, "x"),
        P("x", None),
        P(None, "x"),
        P("x", None),
    )
    return jax.shard_map(shards, mesh=fine, in_specs=in_specs, out_specs=out_specs, check_vma=False)
```

```python
import jax
import jax.numpy as jnp
from jax import lax
from jax.experimental import pallas as pl
from jax.experimental.pallas import tpu as pltpu
from jax.sharding import Mesh, PartitionSpec as P

BF = jnp.bfloat16
F32 = jnp.float32
TABLE = ("zhi", "y", "core")
PLANE = ("y", "core", "x")
COLUMN = ("y", "core")
COLUMN_ORDER = [2, 3, 0, 1]
FAR_FIRST = [5, 4, 7, 6, 1, 0, 3, 2]
TABLE_ORDER = [8 * z + c for z in COLUMN_ORDER for c in FAR_FIRST]
PLANE_ORDER = [4 * c + q for c in FAR_FIRST for q in (2, 3, 0, 1)]
VMEM_BYTES = 48 * 1024 * 1024


def dot(a, b):
    return lax.dot_general(a, b, (((1,), (0,)), ((), ())), preferred_element_type=F32)


def dot_t(a, b):
    return lax.dot_general(a, b, (((1,), (1,)), ((), ())), preferred_element_type=F32)


def params():
    return pltpu.CompilerParams(vmem_limit_bytes=VMEM_BYTES)


def whole(shape):
    zeros = (0,) * len(shape)
    return pl.BlockSpec(shape, lambda i, t: zeros)


def pack_kernel(t_ref, pooled_ref, out_ref, plane_ref):
    row = lax.broadcasted_iota(jnp.int32, (64, 256), 0)
    lane = lax.broadcasted_iota(jnp.int32, (64, 256), 1)
    wanted = 8 * (row % 32) + 2 * t_ref[0] + row // 32
    chosen = jnp.where(lane == wanted, 1.0, 0.0).astype(BF)
    for e in range(8):
        picked = dot_t(chosen, pooled_ref[e])
        first, second = picked[:32], picked[32:]
        plane_ref[0, pl.ds(e, 32, stride=8), :] = first[:, :128]
        plane_ref[1, pl.ds(e, 32, stride=8), :] = second[:, :128]
        plane_ref[2, pl.ds(e, 32, stride=8), :] = jnp.concatenate([first[:, 128:], second[:, 128:]], axis=1)
    rows = jnp.concatenate([plane_ref[i].reshape(32, 8, 128) for i in range(3)], axis=1).astype(BF)
    for k, d in enumerate(TABLE_ORDER):
        out_ref[k] = rows[d]


def pack_rows(t, pooled):
    return pl.pallas_call(
        pack_kernel,
        grid_spec=pltpu.PrefetchScalarGridSpec(
            num_scalar_prefetch=1,
            grid=(1,),
            in_specs=[whole((8, 192, 256))],
            out_specs=whole((32, 24, 128)),
            scratch_shapes=[pltpu.VMEM((3, 256, 128), F32)],
        ),
        out_shape=jax.ShapeDtypeStruct((32, 24, 128), BF),
        compiler_params=params(),
        name="pack_rows",
    )(t, pooled.transpose(1, 2, 0))


def upstream_kernel(t_ref, g_ref, w_ref, ig_ref, igt_ref, base_ref, wt_ref, p_ref):
    lc = w_ref[:, :256]
    pt = w_ref[:, 256:512]
    out_w = w_ref[:, 512:704]
    wt_ref[...] = lc.astype(F32).T.astype(BF)
    p_ref[...] = pt.astype(F32).T.astype(BF)
    for s in range(2):
        g = g_ref[s]
        ig_ref[s] = dot_t(g, out_w).astype(BF)
        igt_ref[s] = dot_t(out_w, g).astype(BF)
        base_ref[s] = g.astype(F32) + dot(lc, g)


def upstream_terms(t, cotangent, weights):
    return pl.pallas_call(
        upstream_kernel,
        grid_spec=pltpu.PrefetchScalarGridSpec(
            num_scalar_prefetch=1,
            grid=(1,),
            in_specs=[
                pl.BlockSpec((2, 256, 192), lambda i, t: (t[0], 0, 0)),
                whole((256, 704)),
            ],
            out_specs=[
                whole((2, 256, 256)),
                whole((2, 256, 256)),
                whole((2, 256, 192)),
                whole((256, 256)),
                whole((256, 256)),
            ],
        ),
        out_shape=[
            jax.ShapeDtypeStruct((2, 256, 256), BF),
            jax.ShapeDtypeStruct((2, 256, 256), BF),
            jax.ShapeDtypeStruct((2, 256, 192), F32),
            jax.ShapeDtypeStruct((256, 256), BF),
            jax.ShapeDtypeStruct((256, 256), BF),
        ],
        compiler_params=params(),
        name="upstream_terms",
    )(t, cotangent, weights)


def layer_kernel(t_ref, x_ref, g_ref, w_ref, ig_ref, igt_ref, base_ref, wt_ref, p_ref, layer_ref, msg_ref):
    pt = w_ref[:, 256:512]
    out_w = w_ref[:, 512:704]
    wt = wt_ref[...]
    planes = x_ref[...].astype(F32)
    planes = jnp.stack([planes[TABLE_ORDER.index(d)] for d in range(32)], axis=0)
    plane = [planes[:, 8 * i : 8 * i + 8].reshape(256, 128) for i in range(3)]
    xs = [
        jnp.concatenate([plane[0], plane[2][:, :64]], axis=1),
        jnp.concatenate([plane[1], plane[2][:, 64:]], axis=1),
    ]
    grads = []
    out_sum = proj_sum = lc_sum = None
    for s in range(2):
        x32 = xs[s]
        x = x32.astype(BF)
        g = g_ref[s]
        ct = dot(pt, x).astype(BF)
        inter = dot_t(x, ct).astype(BF)
        inter_t = dot_t(ct, x).astype(BF)
        forward = dot(inter, out_w) + dot(wt, x)
        layer_ref[s] = (x32 + forward).astype(BF)
        cgt = dot(igt_ref[s], x).astype(BF)
        grads.append(base_ref[s] + dot(ig_ref[s], ct) + dot(p_ref[...], cgt))
        out_term, proj_term, lc_term = dot(inter_t, g), dot_t(cgt, x), dot_t(x, g)
        out_sum = out_term if s == 0 else out_sum + out_term
        proj_sum = proj_term if s == 0 else proj_sum + proj_term
        lc_sum = lc_term if s == 0 else lc_sum + lc_term
    pad = jnp.zeros((256, 32), F32)
    emb = [
        jnp.concatenate([grads[0][:, 48 * q : 48 * q + 48], grads[1][:, 48 * q : 48 * q + 48], pad], axis=1)
        for q in range(4)
    ]
    out_tail = jnp.concatenate([out_sum[:, 128:], jnp.zeros((256, 64), F32)], axis=1)
    for c in range(8):
        for q in range(4):
            rows = slice(64 * q + 8 * c, 64 * q + 8 * c + 8)
            tiles = [emb[q][64 * z + 8 * c : 64 * z + 8 * c + 8] for z in range(4)]
            tiles += [lc_sum[rows, :128], lc_sum[rows, 128:]]
            tiles += [proj_sum[rows, :128], proj_sum[rows, 128:]]
            tiles += [out_sum[rows, :128], out_tail[rows]]
            msg_ref[PLANE_ORDER.index(4 * c + q)] = jnp.concatenate(tiles, axis=0).astype(BF)


def layer_terms(t, rows, cotangent, weights, ig, igt, base, wt, p):
    return pl.pallas_call(
        layer_kernel,
        grid_spec=pltpu.PrefetchScalarGridSpec(
            num_scalar_prefetch=1,
            grid=(1,),
            in_specs=[
                whole((32, 24, 128)),
                pl.BlockSpec((2, 256, 192), lambda i, t: (t[0], 0, 0)),
                whole((256, 704)),
                whole((2, 256, 256)),
                whole((2, 256, 256)),
                whole((2, 256, 192)),
                whole((256, 256)),
                whole((256, 256)),
            ],
            out_specs=[whole((2, 256, 192)), whole((32, 80, 128))],
        ),
        out_shape=[
            jax.ShapeDtypeStruct((2, 256, 192), BF),
            jax.ShapeDtypeStruct((32, 80, 128), BF),
        ],
        compiler_params=params(),
        name="layer_terms",
    )(t, rows, cotangent, weights, ig, igt, base, wt, p)


def weight_kernel(in_ref, out_ref):
    total = in_ref[0, 32:80].astype(F32)
    for d in range(1, 32):
        total = total + in_ref[d, 32:80].astype(F32)
    total = total.astype(BF)
    for r in range(out_ref.shape[0]):
        out_ref[r] = total


def weight_terms(received, rep_count):
    return pl.pallas_call(
        weight_kernel,
        out_shape=jax.ShapeDtypeStruct((rep_count, 48, 128), BF),
        compiler_params=params(),
        name="weight_terms",
    )(received)


def plane_kernel(in_ref, out_ref):
    wide = []
    for c in range(8):
        parts = [in_ref[PLANE_ORDER.index(4 * c + q), 0:32].astype(F32)[:, :96] for q in range(4)]
        wide.append(jnp.concatenate(parts, axis=1))
    for z in range(4):
        rows = jnp.concatenate([wide[c][8 * z : 8 * z + 8] for c in range(8)], axis=0).astype(BF)
        for i in range(3):
            out_ref[z, 64 * i : 64 * i + 64] = rows[:, 128 * i : 128 * i + 128]


def plane_terms(received):
    return pl.pallas_call(
        plane_kernel,
        out_shape=jax.ShapeDtypeStruct((4, 192, 128), BF),
        compiler_params=params(),
        name="plane_terms",
    )(received)


def replica_kernel(weight_ref, emb_ref, out_ref):
    total = weight_ref[0].astype(F32)
    for r in range(1, weight_ref.shape[0]):
        total = total + weight_ref[r].astype(F32)
    total = total.astype(BF)
    for z in range(4):
        out_ref[COLUMN_ORDER.index(z), 0:192] = emb_ref[z]
        out_ref[z, 192:240] = total


def replica_terms(weight, emb):
    return pl.pallas_call(
        replica_kernel,
        out_shape=jax.ShapeDtypeStruct((4, 240, 128), BF),
        compiler_params=params(),
        name="replica_terms",
    )(weight, emb)


def total_kernel(in_ref, out_ref):
    total = in_ref[0, 192:240].astype(F32)
    for z in range(1, 4):
        total = total + in_ref[z, 192:240].astype(F32)
    total = total.astype(BF)
    for c in range(8):
        out_ref[c] = total


def total_terms(received):
    return pl.pallas_call(
        total_kernel,
        out_shape=jax.ShapeDtypeStruct((8, 48, 128), BF),
        compiler_params=params(),
        name="total_terms",
    )(received)


def column_kernel(in_ref, emb_ref):
    for z in range(4):
        planes = [in_ref[COLUMN_ORDER.index(z), 64 * i : 64 * i + 64].astype(F32) for i in range(3)]
        rows = jnp.concatenate(planes, axis=1).reshape(8, 8, 384)
        for i in range(8):
            emb_ref[8 * z : 8 * z + 8, i] = rows[:, :, 48 * i : 48 * i + 48].astype(BF)


def column_terms(received):
    return pl.pallas_call(
        column_kernel,
        out_shape=jax.ShapeDtypeStruct((32, 8, 8, 48), BF),
        compiler_params=params(),
        name="column_terms",
    )(received)


def copy_kernel(in_ref, out_ref):
    out_ref[...] = in_ref[...]


def settle(block):
    return pl.pallas_call(
        copy_kernel,
        out_shape=jax.ShapeDtypeStruct(block.shape, block.dtype),
        compiler_params=params(),
        name="settle",
    )(block)


def final_kernel(wide_scale, out_scale, in_ref, lc_ref, proj_ref, out_ref):
    rows = [in_ref[FAR_FIRST.index(c)].astype(F32) for c in range(8)]
    part = [jnp.concatenate([r[8 * i : 8 * i + 8] for r in rows], axis=0) for i in range(6)]
    lc_ref[...] = jnp.concatenate(part[0:2], axis=1) * wide_scale
    proj_ref[...] = jnp.concatenate(part[2:4], axis=1) * wide_scale
    out_ref[...] = jnp.concatenate([part[4], part[5][:, :64]], axis=1) * out_scale


def final_terms(received, wide_scale, out_scale):
    def kernel(*refs):
        final_kernel(wide_scale, out_scale, *refs)

    return pl.pallas_call(
        kernel,
        out_shape=[
            jax.ShapeDtypeStruct((64, 256), F32),
            jax.ShapeDtypeStruct((64, 256), F32),
            jax.ShapeDtypeStruct((64, 192), F32),
        ],
        compiler_params=params(),
        name="final_terms",
    )(received)


def swap(blocks, axes, order=None):
    groups = None if order is None else [order]
    return lax.all_to_all(blocks, axes, split_axis=0, concat_axis=0, tiled=True, axis_index_groups=groups)


def shards(pooled, lc_weight, fm_proj, fm_out, cotangent):
    t = lax.axis_index("x").astype(jnp.int32)[None]
    rep_count = lax.axis_size("zlo")
    sample_total = cotangent.shape[0] * rep_count * 32
    wide_scale = float(sample_total * 192) ** (-0.5)
    out_scale = float(sample_total * 256 * 192) ** (-0.5)
    middle_first = sorted(range(rep_count), key=lambda r: abs(2 * r - rep_count))
    rows = swap(pack_rows(t, pooled), TABLE, TABLE_ORDER)
    own = jnp.concatenate([lc_weight, fm_proj.T, fm_out], axis=1)
    weights = lax.all_gather(own, "x", axis=0, tiled=True)
    ig, igt, base, wt, p = upstream_terms(t, cotangent, weights)
    layer, messages = layer_terms(t, rows, cotangent, weights, ig, igt, base, wt, p)
    received = swap(messages, PLANE, PLANE_ORDER)
    weight = swap(weight_terms(received, rep_count), "zlo", middle_first)
    column = swap(replica_terms(weight, plane_terms(received)), "zhi", COLUMN_ORDER)
    layer_out = settle(lax.all_gather(layer.transpose(0, 2, 1), "x", axis=0, tiled=True))
    column, _ = lax.optimization_barrier((column, layer_out))
    total = swap(total_terms(column), COLUMN, FAR_FIRST)
    emb_grad = column_terms(column)
    lc_grad, proj_grad, out_grad = final_terms(total, wide_scale, out_scale)
    return (layer_out.transpose(0, 2, 1), emb_grad.reshape(256, 8, 48), lc_grad, proj_grad.T, out_grad)


def solution(mesh):
    reps = mesh.shape["rep"]
    fine = Mesh(mesh.devices.reshape(reps, 4, 4, 2, 4), ("zlo", "zhi", "y", "core", "x"))
    in_specs = (
        P("zlo", TABLE, None),
        P("x", None),
        P(None, "x"),
        P("x", None),
        P(("zlo",) + TABLE, None, None),
    )
    out_specs = (
        P(("zlo",) + TABLE, None, None),
        P("zlo", TABLE, "x"),
        P("x", None),
        P(None, "x"),
        P("x", None),
    )
    return jax.shard_map(shards, mesh=fine, in_specs=in_specs, out_specs=out_specs, check_vma=False)
```
